128 devices in a mesh: parts: 128 (over z, y, x, core).
Axes of the slice: x: 4, y: 4, z: 4, core: 2. Of those that a mesh axis runs over, the one named last changes fastest.
Arguments:
- start_vectors: float32 [2097152, 16], P('parts'), may hold values from -120 to 120
- tile_index: int32 [32768, 2], P('parts'), may hold values from 0 to 255, as said below
- tile_values: bfloat16 [32768, 128, 128], P('parts'), may hold values from 0 to 1
- tile_count: int32 [128], P('parts'), may hold values from 128 to 256, as said below
- ghost_send: int32 [128, 2, 64], P('parts'), may hold values from 0 to 127, as said below
Outputs:
- basis_out: float32 [2097152, 80], P('parts')
- gram_matrix: float32 [80, 80], replicated
The draws below stay inside these ranges and needn't reach their ends.
Inputs may be any that keep to these rules, and one draw needn't show every extreme that they name: `tile_index`: column 0 is a row block of the part, column 1 a block of its extended region; among a part's first 128 slots every one of the 128 ghost blocks is named exactly once and the other slots name own blocks. `tile_count`: slots at or beyond a part's count are dead; some part uses all 256 slots. `ghost_send`: each list holds distinct own block indices.
All inputs are finite; a program needn't handle non-finite values.
Results may differ from the reference program's by a relative error of at most 0.0058.
Values may be sent and summed in bfloat16 or wider, within the bound.
No kernel may reach another device: no remote copies, remote signals or barrier semaphores. Data moves between devices by JAX's collectives and lax.ppermute only.
A program may use at most 128 MiB of HBM per device.

```python
import jax
import jax.numpy as jnp
from jax import lax

BLK = 16
STEPS = 4
TILE = 128
BASIS = 80
RB = 128
GHOST = 64
NT = 256
NROWS = 2097152
NTOT = 32768
N_PARTS = 128


def draw_start_vectors(key, part):
    key = jax.random.fold_in(key, 11)
    subkeys = jax.random.split(key, 3)
    position = jnp.arange(NROWS, dtype=jnp.float32) / NROWS
    rising = jnp.exp(jnp.log(3.0) * position)
    row_scale = jnp.exp(jax.random.uniform(subkeys[0], (NROWS,), minval=0.0, maxval=jnp.log(10.0)))
    col_scale = jnp.exp(jax.random.uniform(subkeys[1], (BLK,), minval=0.0, maxval=jnp.log(10.0)))
    values_base = jnp.clip(jax.random.normal(subkeys[2], (NROWS, BLK)), -4.0, 4.0)
    return (values_base * (rising * row_scale)[:, None] * col_scale[None, :] * 0.1).astype(jnp.float32)


def draw_tile_values(key, part):
    key = jax.random.fold_in(key, 13)
    subkeys = jax.random.split(key, 2)
    kept = jax.random.uniform(subkeys[0], (NTOT, TILE, TILE)) < 0.125
    weights = jnp.exp(jax.random.uniform(subkeys[1], (NTOT, TILE, TILE), minval=jnp.log(0.1), maxval=0.0))
    return jnp.where(kept, weights, 0.0).astype(jnp.bfloat16)


def draw_tile_index(key, part):
    key = jax.random.fold_in(key, 5)
    subkeys = jax.random.split(key, 3)
    row_blocks = jax.random.randint(subkeys[0], (N_PARTS, NT), 0, RB)
    slot_index = jnp.arange(NT)[None, :]
    own_cols = jax.random.randint(subkeys[1], (N_PARTS, NT), 0, RB)
    columns = jnp.where(slot_index < 2 * GHOST, RB + slot_index, own_cols)
    half_tiles = NT // 2
    shuffles = jax.vmap(lambda sub: jax.random.permutation(sub, half_tiles))(jax.random.split(subkeys[2], N_PARTS))
    first_half = jnp.take_along_axis(columns[:, :half_tiles], shuffles, axis=1)
    columns = jnp.concatenate([first_half, columns[:, half_tiles:]], 1)
    return jnp.stack([row_blocks, columns], -1).reshape(NTOT, 2).astype(jnp.int32)


def draw_tile_count(key, part):
    key = jax.random.fold_in(key, 7)
    subkeys = jax.random.split(key, 2)
    counts = jax.random.randint(subkeys[0], (N_PARTS,), NT // 2, NT + 1)
    busiest = jax.random.randint(subkeys[1], (), 0, N_PARTS)
    return jnp.where(jnp.arange(N_PARTS) == busiest, NT, counts).astype(jnp.int32)


def draw_ghost_send(key, part):
    key = jax.random.fold_in(key, 9)
    shuffles = jax.vmap(lambda sub: jax.random.permutation(sub, RB))(jax.random.split(key, 2 * N_PARTS))
    return shuffles[:, :GHOST].reshape(N_PARTS, 2, GHOST).astype(jnp.int32)


def setup_inputs(seed: int = 0) -> dict:
    streams_of = jax.random.split(jax.random.key(seed), 6)
    start_vectors = draw_start_vectors(jax.random.fold_in(streams_of[5], 71), 0)
    tile_index = draw_tile_index(jax.random.fold_in(streams_of[5], 71), 0)
    tile_values = draw_tile_values(jax.random.fold_in(streams_of[5], 71), 0)
    tile_count = draw_tile_count(jax.random.fold_in(streams_of[5], 71), 0)
    ghost_send = draw_ghost_send(jax.random.fold_in(streams_of[5], 71), 0)
    return dict(start_vectors=start_vectors, tile_index=tile_index, tile_values=tile_values, tile_count=tile_count, ghost_send=ghost_send)


PRECISE = lax.Precision.HIGHEST

def block_onehot(tile_pairs, live_count, block_total):
    live_mask = jnp.arange(tile_pairs.shape[0]) < live_count
    return ((tile_pairs[:, 0][None, :] == jnp.arange(block_total)[:, None]) & live_mask[None, :]).astype(jnp.float32)

def part_degree(packed):
    tile_blocks, tile_pairs, live_count = packed
    onehot = block_onehot(tile_pairs, live_count, RB)
    sums = lax.optimization_barrier(jnp.sum(tile_blocks, axis=2, dtype=jnp.float32))
    return 1.0 + jnp.dot(onehot.astype(jnp.float32), sums.astype(jnp.float32), precision=PRECISE, preferred_element_type=jnp.float32)

def part_product(packed):
    own_blocks, prev_blocks, next_blocks, prev_list, next_list, tile_blocks, tile_pairs, live_count = packed
    extended = jnp.concatenate([own_blocks, prev_blocks[prev_list], next_blocks[next_list]], 0)
    operands = extended[tile_pairs[:, 1]].astype(jnp.float32)
    products = jnp.einsum('tij,tjc->tic', tile_blocks.astype(jnp.float32), operands, precision=PRECISE)
    onehot = block_onehot(tile_pairs, live_count, own_blocks.shape[0])
    return jnp.einsum('rt,tic->ric', onehot, products, precision=PRECISE)

def reference(start_vectors, tile_index, tile_values, tile_count, ghost_send):
    tile_pairs = tile_index.reshape(N_PARTS, NT, 2)
    tile_blocks = tile_values.reshape(N_PARTS, NT, TILE, TILE)
    degree = lax.map(part_degree, (tile_blocks, tile_pairs, tile_count)).reshape(NROWS)
    row_scale = (1.0 / jnp.sqrt(degree))[:, None]
    prev_lists = jnp.roll(ghost_send[:, 0], 1, axis=0)
    next_lists = jnp.roll(ghost_send[:, 1], -1, axis=0)

    def spread(vector_in):
        scaled = (row_scale * vector_in).astype(jnp.bfloat16).reshape(N_PARTS, RB, TILE, BLK)
        summed = lax.map(part_product, (scaled, jnp.roll(scaled, 1, 0), jnp.roll(scaled, -1, 0), prev_lists, next_lists, tile_blocks, tile_pairs, tile_count))
        return row_scale * summed.reshape(NROWS, BLK)
    vectors = [start_vectors]
    for hop_number in range(STEPS):
        applied = spread(vectors[-1])
        if hop_number == 0:
            vectors.append(applied)
        else:
            vectors.append(2.0 * applied - vectors[-2])
    krylov = jnp.concatenate(vectors, 1)
    gram_matrix = jnp.dot(krylov.T.astype(jnp.float32), krylov.astype(jnp.float32), precision=PRECISE, preferred_element_type=jnp.float32) / NROWS
    factor = jnp.linalg.cholesky(gram_matrix)
    inverse = jax.scipy.linalg.solve_triangular(factor, jnp.eye(BASIS, dtype=jnp.float32), lower=True)
    basis_out = jnp.dot(krylov.astype(jnp.float32), inverse.T.astype(jnp.float32), precision=PRECISE, preferred_element_type=jnp.float32)
    return (basis_out, gram_matrix)
```

```python
import functools

import jax
import jax.numpy as jnp
from jax import lax
from jax.experimental import pallas as pl
from jax.experimental.pallas import tpu as pltpu
from jax.sharding import PartitionSpec as P

STEPS = 4
AXIS = "parts"
VMEM = pltpu.VMEM
SMEM = pltpu.SMEM
F32 = jnp.float32
BF16 = jnp.bfloat16

SLOT, GROW, OCOL, OROW, SEND = range(5)


def spec(space):
    return pl.BlockSpec(memory_space=space)


def tile_product(block, tile):
    return lax.dot_general(block, tile, (((1,), (1,)), ((), ())), preferred_element_type=F32)


def pack(plan_ref, scaled_ref, send_a_ref, send_b_ref):
    half = send_a_ref.shape[0]

    def step(base, _):
        for u in range(8):
            g = base * 8 + u
            send_b_ref[g] = scaled_ref[plan_ref[SEND, half + g]]
        for u in range(8):
            g = base * 8 + u
            send_a_ref[g] = scaled_ref[plan_ref[SEND, g]]
        return 0

    lax.fori_loop(0, half // 8, step, 0)


def setup_kernel(index_ref, count_ref, ghost_ref, values_ref, start_ref,
                 tiles_ref, plan_ref, scale_ref, scaled_ref, send_a_ref, send_b_ref,
                 acc_ref, sems):
    total, side = values_ref.shape[0], values_ref.shape[1]
    blocks = scaled_ref.shape[0]
    half = send_a_ref.shape[0]
    ghosts = 2 * half
    chunks = sems.shape[0]
    per = total // chunks

    def copy(k):
        return pltpu.make_async_copy(
            values_ref.at[pl.ds(k * per, per)], tiles_ref.at[pl.ds(k * per, per)], sems.at[k]
        )

    for k in range(chunks):
        copy(k).start()

    odd = lax.rem(lax.axis_index(AXIS), 2)
    flip = (1 - odd) * half
    count = count_ref[0]
    acc_ref[...] = jnp.zeros_like(acc_ref)

    def ghost_plan(base, _):
        for u in range(4):
            t = base * 4 + u
            place = jnp.bitwise_xor(index_ref[1, t] - blocks, flip)
            plan_ref[SLOT, place] = t
            plan_ref[GROW, place] = index_ref[0, t]
            plan_ref[OCOL, t] = index_ref[1, ghosts + t]
            plan_ref[OROW, t] = jnp.where(ghosts + t < count, index_ref[0, ghosts + t], blocks)
        return 0

    lax.fori_loop(0, ghosts // 4, ghost_plan, 0)

    def send_plan(g, _):
        plan_ref[SEND, g] = ghost_ref[odd, g]
        plan_ref[SEND, half + g] = ghost_ref[1 - odd, g]
        return 0

    lax.fori_loop(0, half, send_plan, 0)

    ones = jnp.ones((16, side), BF16)
    for k in range(chunks):
        copy(k).wait()

        def degree_step(base, _):
            for u in range(8):
                t = k * per + base * 8 + u
                row = jnp.where(t < count, index_ref[0, t], blocks)
                acc_ref[row] += tile_product(ones, tiles_ref[t])
            return 0

        lax.fori_loop(0, per // 8, degree_step, 0)

    def scale_step(base, _):
        for u in range(8):
            b = base * 8 + u
            factor = 1.0 / jnp.sqrt(1.0 + acc_ref[b])
            scale_ref[b] = factor
            at = pl.ds(pl.multiple_of(b * side, side), side)
            scaled_ref[b] = (factor * start_ref[:, at]).astype(BF16)
        return 0

    lax.fori_loop(0, blocks // 8, scale_step, 0)
    pack(plan_ref, scaled_ref, send_a_ref, send_b_ref)


def split(value):
    high = value.astype(BF16)
    return high, (value - high.astype(F32)).astype(BF16)


def gram_rows(parts, gram_ref, level):
    rows = parts[0].shape[1]
    chunk = 1024
    width = 16 * (level + 1)
    acc = jnp.zeros((32, 2 * width), F32)
    for k in range(rows // chunk):
        at = slice(k * chunk, (k + 1) * chunk)
        right = jnp.concatenate([p[:16, at] for p in parts] + [p[16:, at] for p in parts], 0)
        acc += lax.dot_general(parts[-1][:, at], right, (((1,), (1,)), ((), ())), preferred_element_type=F32)
    both = acc[:16] + acc[16:]
    gram_ref[16 * level:16 * (level + 1), :width] = both[:, :width] + both[:, width:]


def own_kernel(level, *refs):
    plan_ref, tiles_ref, scaled_ref, got_ref, vec_ref = refs[:5]
    older = refs[5:5 + level]
    at = 5 + level
    gram_in = None
    if level:
        gram_in = refs[at]
        at += 1
    acc_ref, part_ref, gram_ref = refs[at:at + 3]
    half = got_ref.shape[0]
    acc_ref[...] = jnp.zeros_like(acc_ref)
    ghosts = 2 * half

    def own_step(base, _):
        for u in range(8):
            t = base * 8 + u
            acc_ref[plan_ref[OROW, t]] += tile_product(
                scaled_ref[plan_ref[OCOL, t]], tiles_ref[ghosts + t])
        return 0

    lax.fori_loop(0, ghosts // 8, own_step, 0)

    def near_step(base, _):
        for u in range(8):
            g = base * 8 + u
            acc_ref[plan_ref[GROW, g]] += tile_product(got_ref[g], tiles_ref[plan_ref[SLOT, g]])
        return 0

    lax.fori_loop(0, half // 8, near_step, 0)

    high, low = split(vec_ref[...])
    part_ref[:16] = high
    part_ref[16:] = low
    gram_ref[...] = gram_in[...] if level else jnp.zeros_like(gram_ref)
    gram_rows(tuple(older) + (part_ref,), gram_ref, level)


def far_kernel(level, last, *refs):
    plan_ref, tiles_ref, got_ref, acc_in, scale_ref = refs[:5]
    at = 5
    prev_ref = None
    if level > 1:
        prev_ref = refs[at]
        at += 1
    if last:
        older = refs[at:at + level]
        gram_in = refs[at + level]
        at += level + 1
        part_ref, gram_ref, acc_ref = refs[at:at + 3]
    else:
        vec_ref, scaled_ref, send_a_ref, send_b_ref, acc_ref = refs[at:at + 5]
    half = got_ref.shape[0]
    side = tiles_ref.shape[1]
    blocks = scale_ref.shape[0]
    acc_ref[...] = acc_in[...]

    def far_step(base, _):
        for u in range(8):
            g = base * 8 + u
            acc_ref[plan_ref[GROW, half + g]] += tile_product(
                got_ref[g], tiles_ref[plan_ref[SLOT, half + g]])
        return 0

    lax.fori_loop(0, half // 8, far_step, 0)

    def close_step(base, _):
        for u in range(8):
            b = base * 8 + u
            where = pl.ds(pl.multiple_of(b * side, side), side)
            factor = scale_ref[b]
            value = factor * acc_ref[b]
            if level > 1:
                value = 2.0 * value - prev_ref[:, where]
            if last:
                high, low = split(value)
                part_ref[:16, where] = high
                part_ref[16:, where] = low
            else:
                vec_ref[:, where] = value
                scaled_ref[b] = (factor * value).astype(BF16)
        return 0

    lax.fori_loop(0, blocks // 8, close_step, 0)
    if last:
        gram_ref[...] = gram_in[...]
        gram_rows(tuple(older) + (part_ref,), gram_ref, level)
    else:
        pack(plan_ref, scaled_ref, send_a_ref, send_b_ref)


def inverse_factor(gram):
    size = gram.shape[0]
    row = lax.broadcasted_iota(jnp.int32, gram.shape, 0)
    lane = lax.broadcasted_iota(jnp.int32, gram.shape, 1)
    left, right = gram, jnp.where(row == lane, 1.0, 0.0)
    row8 = lax.broadcasted_iota(jnp.int32, (8, 128), 0)
    done = []
    for base in range(0, size, 8):
        a, b = left[:8], right[:8]
        for j in range(8):
            at = base + j
            scale = lax.rsqrt(a[j:j + 1, at:at + 1])
            line_a, line_b = a[j:j + 1] * scale, b[j:j + 1] * scale
            column = jnp.where(row8 > j, a[:, at:at + 1] * scale, 0.0)
            a = jnp.where(row8 == j, line_a, a - column * line_a)
            b = jnp.where(row8 == j, line_b, b - column * line_b)
        done.append(b)
        if base + 8 < size:
            both = jnp.concatenate([a, b], 1)
            change = lax.dot_general(
                a.T[base + 8:size], both, (((1,), (0,)), ((), ())),
                precision=lax.Precision.HIGHEST, preferred_element_type=F32)
            left = left[8:] - change[:, :128]
            right = right[8:] - change[:, 128:]
    return jnp.concatenate(done, 0)


def final_kernel(row_total, gram_in, *refs):
    parts = refs[:STEPS + 1]
    basis_ref, gram_ref, mix_ref = refs[STEPS + 1:]
    width = gram_ref.shape[0]
    chunk = basis_ref.shape[1]

    @pl.when(pl.program_id(0) == 0)
    def _():
        lower = gram_in[...] * (1.0 / row_total)
        row = lax.broadcasted_iota(jnp.int32, lower.shape, 0)
        lane = lax.broadcasted_iota(jnp.int32, lower.shape, 1)
        lower = jnp.where(row >= lane, lower, 0.0)
        strict = jnp.where(row > lane, lower, 0.0)
        square = jnp.concatenate([strict, jnp.zeros((128 - width, 128), F32)], 0)
        full = lower + square.T[:width]
        gram_ref[...] = full[:, :width]
        inverse = inverse_factor(full)
        high, low = split(inverse[:, :width])
        mix_ref[...] = jnp.concatenate([high, low, high], 1)

    at = pl.ds(pl.multiple_of(pl.program_id(0) * chunk, chunk), chunk)
    tops = [p[:16, at] for p in parts]
    lows = [p[16:, at] for p in parts]
    stack = jnp.concatenate(tops + tops + lows, 0)
    basis_ref[...] = jnp.dot(mix_ref[...], stack, preferred_element_type=F32)


def params(mib, **kw):
    return pltpu.CompilerParams(vmem_limit_bytes=mib * 2**20, **kw)


def body(start_vectors, tile_index, tile_values, tile_count, ghost_send):
    rows, width = start_vectors.shape
    total, side, _ = tile_values.shape
    blocks = rows // side
    half = ghost_send.shape[2]
    n = lax.axis_size(AXIS)
    basis = width * (STEPS + 1)
    shape = jax.ShapeDtypeStruct

    scaled_t = shape((blocks, width, side), BF16)
    send_t = shape((half, width, side), BF16)
    vec_t = shape((width, rows), F32)
    part_t = shape((2 * width, rows), BF16)
    acc_t = shape((blocks + 1, width, side), F32)
    gram_t = shape((basis, 128), F32)

    near = [(i, i ^ 1) for i in range(n)]
    far = [(i, (i + 1) % n if i % 2 else (i - 1) % n) for i in range(n)]

    start = start_vectors.T
    tiles, plan, scale, scaled, send_a, send_b = pl.pallas_call(
        setup_kernel,
        out_shape=(shape((total, side, side), BF16), shape((8, 128), jnp.int32),
                   shape((blocks, width, side), F32), scaled_t, send_t, send_t),
        in_specs=[spec(SMEM), spec(SMEM), spec(SMEM), spec(pltpu.HBM), spec(VMEM)],
        out_specs=(spec(VMEM), spec(SMEM), spec(VMEM), spec(VMEM), spec(VMEM), spec(VMEM)),
        scratch_shapes=[VMEM(acc_t.shape, F32), pltpu.SemaphoreType.DMA((16,))],
        compiler_params=params(20),
        name="setup",
    )(tile_index.T, tile_count, ghost_send[0], tile_values, start)

    vectors = [start]
    parts = []
    gram = None
    for level in range(1, STEPS + 1):
        last = level == STEPS
        got_b = lax.ppermute(send_b, AXIS, far)
        got_a = lax.ppermute(send_a, AXIS, near)
        args = [plan, tiles, scaled, got_a, vectors[-1]] + parts + ([gram] if gram is not None else [])
        acc, part, gram = pl.pallas_call(
            functools.partial(own_kernel, level - 1),
            out_shape=(acc_t, part_t, gram_t),
            in_specs=[spec(SMEM)] + [spec(VMEM)] * (len(args) - 1),
            out_specs=(spec(VMEM),) * 3,
            compiler_params=params(20),
            cost_estimate=pl.CostEstimate(flops=10**9, bytes_accessed=10**7, transcendentals=0),
            name="own",
        )(*args)
        parts.append(part)
        args = [plan, tiles, got_b, acc, scale]
        if level > 1:
            args.append(vectors[-2])
        if last:
            args += parts + [gram]
            outs = (part_t, gram_t)
        else:
            outs = (vec_t, scaled_t, send_t, send_t)
        got = pl.pallas_call(
            functools.partial(far_kernel, level, last),
            out_shape=outs,
            in_specs=[spec(SMEM)] + [spec(VMEM)] * (len(args) - 1),
            out_specs=(spec(VMEM),) * len(outs),
            scratch_shapes=[VMEM(acc_t.shape, F32)],
            compiler_params=params(20),
            name="far",
        )(*args)
        if last:
            part, gram = got
            parts.append(part)
        else:
            vec, scaled, send_a, send_b = got
            vectors.append(vec)

    def phase(value, shift, count):
        mask = (count - 1) << shift
        moved = value
        for d in range(1, count):
            perm = [(i, (i & ~mask) | ((((i >> shift) + d) & (count - 1)) << shift)) for i in range(n)]
            moved = moved + lax.ppermute(value, AXIS, perm)
        return moved

    for shift, count in ((0, 2), (1, 4), (3, 4), (5, 4)):
        gram = phase(gram, shift, count)

    chunk = 1024
    basis_out, gram_matrix = pl.pallas_call(
        functools.partial(final_kernel, rows * n),
        grid=(rows // chunk,),
        out_shape=(shape((basis, rows), F32), shape((basis, basis), F32)),
        in_specs=[spec(VMEM)] * (STEPS + 2),
        out_specs=(pl.BlockSpec((basis, chunk), lambda i: (0, i)),
                   pl.BlockSpec((basis, basis), lambda i: (0, 0))),
        scratch_shapes=[VMEM((basis, 3 * basis), BF16)],
        compiler_params=params(20),
        name="final",
    )(gram, *parts)
    return basis_out.T, gram_matrix


def solution(mesh):
    placed = (
        P("parts", None),
        P("parts", None),
        P("parts", None, None),
        P("parts"),
        P("parts", None, None),
    )
    return jax.shard_map(
        body, mesh=mesh, in_specs=placed, out_specs=(P("parts", None), P()), check_vma=False
    )
```

```python
import functools

import jax
import jax.numpy as jnp
from jax import lax
from jax.experimental import pallas as pl
from jax.experimental.pallas import tpu as pltpu
from jax.sharding import PartitionSpec as P

STEPS = 4
AXIS = "parts"
VMEM = pltpu.VMEM
SMEM = pltpu.SMEM
F32 = jnp.float32
BF16 = jnp.bfloat16

SLOT, GROW, OCOL, OROW, SEND = range(5)


def spec(space):
    return pl.BlockSpec(memory_space=space)


def tile_product(block, tile):
    return lax.dot_general(block, tile, (((1,), (1,)), ((), ())), preferred_element_type=F32)


def quad_products(blocks, tiles):
    zero = jnp.zeros_like(blocks[0])
    join = jnp.concatenate
    out = []
    for i in range(0, len(blocks), 4):
        x, t = blocks[i:i + 4], tiles[i:i + 4]
        left = join([join([x[0], zero], 1), join([zero, x[1]], 1), join([x[2], zero], 1), join([zero, x[3]], 1)], 0)
        right = join([join([t[0], t[1]], 1), join([t[2], t[3]], 1)], 0)
        got = tile_product(left, right)
        out += [got[:16, :128], got[16:32, :128], got[32:48, 128:], got[48:, 128:]]
    return out


def spread_tiles(count, unroll, acc_ref, block_at, tile_at, row_at):
    def step(base, _):
        at = [base * unroll + u for u in range(unroll)]
        got = quad_products([block_at(t) for t in at], [tile_at(t) for t in at])
        for t, product in zip(at, got):
            acc_ref[row_at(t)] += product
        return 0

    lax.fori_loop(0, count // unroll, step, 0)


def pack(plan_ref, scaled_ref, send_a_ref, send_b_ref):
    half = send_a_ref.shape[0]

    def step(base, _):
        for u in range(8):
            g = base * 8 + u
            send_b_ref[g] = scaled_ref[plan_ref[SEND, half + g]]
        for u in range(8):
            g = base * 8 + u
            send_a_ref[g] = scaled_ref[plan_ref[SEND, g]]
        return 0

    lax.fori_loop(0, half // 8, step, 0)


def setup_kernel(index_ref, count_ref, ghost_ref, values_ref, start_ref,
                 tiles_ref, plan_ref, scale_ref, scaled_ref, send_a_ref, send_b_ref,
                 acc_ref, sems):
    total, side = values_ref.shape[0], values_ref.shape[1]
    blocks = scaled_ref.shape[0]
    half = send_a_ref.shape[0]
    ghosts = 2 * half
    chunks = sems.shape[0]
    per = total // chunks

    def copy(k):
        return pltpu.make_async_copy(
            values_ref.at[pl.ds(k * per, per)], tiles_ref.at[pl.ds(k * per, per)], sems.at[k]
        )

    for k in range(chunks):
        copy(k).start()

    odd = lax.rem(lax.axis_index(AXIS), 2)
    flip = (1 - odd) * half
    count = count_ref[0]
    acc_ref[...] = jnp.zeros_like(acc_ref)

    def ghost_plan(base, _):
        for u in range(4):
            t = base * 4 + u
            place = jnp.bitwise_xor(index_ref[1, t] - blocks, flip)
            plan_ref[SLOT, place] = t
            plan_ref[GROW, place] = index_ref[0, t]
            plan_ref[OCOL, t] = index_ref[1, ghosts + t]
            plan_ref[OROW, t] = jnp.where(ghosts + t < count, index_ref[0, ghosts + t], blocks)
        return 0

    lax.fori_loop(0, ghosts // 4, ghost_plan, 0)

    def send_plan(g, _):
        plan_ref[SEND, g] = ghost_ref[odd, g]
        plan_ref[SEND, half + g] = ghost_ref[1 - odd, g]
        return 0

    lax.fori_loop(0, half, send_plan, 0)

    row = lax.broadcasted_iota(jnp.int32, (16, 2 * side), 0)
    lane = lax.broadcasted_iota(jnp.int32, (16, 2 * side), 1)
    ones = jnp.where((row < 8) == (lane < side), 1.0, 0.0).astype(BF16)
    join = jnp.concatenate
    for k in range(chunks):
        copy(k).wait()
        slots = [k * per + u for u in range(per)]
        got = []
        for i in range(0, per, 4):
            t = [tiles_ref[slot] for slot in slots[i:i + 4]]
            sums = tile_product(ones, join([join([t[0], t[1]], 1), join([t[2], t[3]], 1)], 0))
            got += [sums[:8, :side], sums[8:, :side], sums[:8, side:], sums[8:, side:]]
        for t, part in zip(slots, got):
            target = index_ref[0, t]
            if t >= ghosts:
                target = jnp.where(t < count, target, blocks)
            acc_ref[target] += part

    def scale_step(base, _):
        for u in range(8):
            b = base * 8 + u
            factor = lax.rsqrt(1.0 + acc_ref[b])
            scale_ref[b] = factor
            at = pl.ds(pl.multiple_of(b * side, side), side)
            scaled_ref[b] = (join([factor, factor], 0) * start_ref[:, at]).astype(BF16)
        return 0

    lax.fori_loop(0, blocks // 8, scale_step, 0)
    pack(plan_ref, scaled_ref, send_a_ref, send_b_ref)


def split(value):
    high = value.astype(BF16)
    return high, (value - high.astype(F32)).astype(BF16)


def gram_rows(parts, gram_ref, level):
    rows = parts[0].shape[1]
    chunk = 1024
    width = 16 * (level + 1)
    acc = jnp.zeros((32, 2 * width), F32)
    for k in range(rows // chunk):
        at = slice(k * chunk, (k + 1) * chunk)
        right = jnp.concatenate([p[:16, at] for p in parts] + [p[16:, at] for p in parts], 0)
        acc += lax.dot_general(parts[-1][:, at], right, (((1,), (1,)), ((), ())), preferred_element_type=F32)
    both = acc[:16] + acc[16:]
    gram_ref[16 * level:16 * (level + 1), :width] = both[:, :width] + both[:, width:]


def own_kernel(level, *refs):
    plan_ref, tiles_ref, scaled_ref, got_ref, vec_ref = refs[:5]
    older = refs[5:5 + level]
    at = 5 + level
    gram_in = None
    if level:
        gram_in = refs[at]
        at += 1
    acc_ref, part_ref, gram_ref = refs[at:at + 3]
    half = got_ref.shape[0]
    acc_ref[...] = jnp.zeros_like(acc_ref)
    ghosts = 2 * half

    spread_tiles(ghosts, 32, acc_ref, lambda t: scaled_ref[plan_ref[OCOL, t]],
                 lambda t: tiles_ref[ghosts + t], lambda t: plan_ref[OROW, t])
    spread_tiles(half, 32, acc_ref, lambda g: got_ref[g],
                 lambda g: tiles_ref[plan_ref[SLOT, g]], lambda g: plan_ref[GROW, g])
    high, low = split(vec_ref[...])
    part_ref[:16] = high
    part_ref[16:] = low
    gram_ref[...] = gram_in[...] if level else jnp.zeros_like(gram_ref)
    gram_rows(tuple(older) + (part_ref,), gram_ref, level)


def far_kernel(level, last, *refs):
    plan_ref, tiles_ref, got_ref, _, scale_ref = refs[:5]
    at = 5
    prev_ref = None
    if level > 1:
        prev_ref = refs[at]
        at += 1
    if last:
        older = refs[at:at + level]
        gram_in = refs[at + level]
        at += level + 1
        part_ref, gram_ref, acc_ref = refs[at:at + 3]
    else:
        vec_ref, scaled_ref, send_a_ref, send_b_ref, acc_ref = refs[at:at + 5]
    half = got_ref.shape[0]
    side = tiles_ref.shape[1]
    blocks = scale_ref.shape[0]
    spread_tiles(half, 32, acc_ref, lambda g: got_ref[g],
                 lambda g: tiles_ref[plan_ref[SLOT, half + g]], lambda g: plan_ref[GROW, half + g])

    def close_step(base, _):
        for u in range(8):
            b = base * 8 + u
            where = pl.ds(pl.multiple_of(b * side, side), side)
            factor = jnp.concatenate([scale_ref[b], scale_ref[b]], 0)
            value = factor * acc_ref[b]
            if level > 1:
                value = 2.0 * value - prev_ref[:, where]
            if last:
                high, low = split(value)
                part_ref[:16, where] = high
                part_ref[16:, where] = low
            else:
                vec_ref[:, where] = value
                scaled_ref[b] = (factor * value).astype(BF16)
        return 0

    lax.fori_loop(0, blocks // 8, close_step, 0)
    if last:
        gram_ref[...] = gram_in[...]
        gram_rows(tuple(older) + (part_ref,), gram_ref, level)
    else:
        pack(plan_ref, scaled_ref, send_a_ref, send_b_ref)


def inverse_factor(gram):
    size = gram.shape[0]
    row = lax.broadcasted_iota(jnp.int32, gram.shape, 0)
    lane = lax.broadcasted_iota(jnp.int32, gram.shape, 1)
    left, right = gram, jnp.where(row == lane, 1.0, 0.0)
    row8 = lax.broadcasted_iota(jnp.int32, (8, 128), 0)
    done = []
    for base in range(0, size, 8):
        a, b = left[:8], right[:8]
        for j in range(8):
            at = base + j
            scale = lax.rsqrt(a[j:j + 1, at:at + 1])
            line_a, line_b = a[j:j + 1] * scale, b[j:j + 1] * scale
            column = jnp.where(row8 > j, a[:, at:at + 1] * scale, 0.0)
            a = jnp.where(row8 == j, line_a, a - column * line_a)
            b = jnp.where(row8 == j, line_b, b - column * line_b)
        done.append(b)
        if base + 8 < size:
            both = jnp.concatenate([a, b], 1)
            change = lax.dot_general(
                a.T[base + 8:size], both, (((1,), (0,)), ((), ())),
                precision=lax.Precision.HIGHEST, preferred_element_type=F32)
            left = left[8:] - change[:, :128]
            right = right[8:] - change[:, 128:]
    return jnp.concatenate(done, 0)


def final_kernel(row_total, gram_in, *refs):
    parts = refs[:STEPS + 1]
    basis_ref, gram_ref, mix_ref, stage_ref, sems = refs[STEPS + 1:]
    width = gram_ref.shape[0]

    if True:
        lower = gram_in[...] * (1.0 / row_total)
        row = lax.broadcasted_iota(jnp.int32, lower.shape, 0)
        lane = lax.broadcasted_iota(jnp.int32, lower.shape, 1)
        lower = jnp.where(row >= lane, lower, 0.0)
        strict = jnp.where(row > lane, lower, 0.0)
        square = jnp.concatenate([strict, jnp.zeros((128 - width, 128), F32)], 0)
        full = lower + square.T[:width]
        gram_ref[...] = full[:, :width]
        inverse = inverse_factor(full)
        high, low = split(inverse[:, :width])
        mix_ref[...] = jnp.concatenate([high, low, high], 1)

    pieces = stage_ref.shape[0]
    chunk = stage_ref.shape[2]

    def out(k):
        return pltpu.make_async_copy(stage_ref.at[k], basis_ref.at[:, pl.ds(k * chunk, chunk)], sems.at[k])

    mix = mix_ref[...]
    for k in range(pieces):
        at = slice(k * chunk, (k + 1) * chunk)
        tops = [p[:16, at] for p in parts]
        lows = [p[16:, at] for p in parts]
        stack = jnp.concatenate(tops + tops + lows, 0)
        stage_ref[k] = jnp.dot(mix, stack, preferred_element_type=F32)
        out(k).start()
    for k in range(pieces):
        out(k).wait()


def params(mib, **kw):
    return pltpu.CompilerParams(vmem_limit_bytes=mib * 2**20, **kw)


def body(start_vectors, tile_index, tile_values, tile_count, ghost_send):
    rows, width = start_vectors.shape
    total, side, _ = tile_values.shape
    blocks = rows // side
    half = ghost_send.shape[2]
    n = lax.axis_size(AXIS)
    basis = width * (STEPS + 1)
    shape = jax.ShapeDtypeStruct

    scaled_t = shape((blocks, width, side), BF16)
    send_t = shape((half, width, side), BF16)
    vec_t = shape((width, rows), F32)
    part_t = shape((2 * width, rows), BF16)
    acc_t = shape((blocks + 1, width, side), F32)
    gram_t = shape((basis, 128), F32)

    near = [(i, i ^ 1) for i in range(n)]
    far = [(i, (i + 1) % n if i % 2 else (i - 1) % n) for i in range(n)]

    start = start_vectors.T
    tiles, plan, scale, scaled, send_a, send_b = pl.pallas_call(
        setup_kernel,
        out_shape=(shape((total, side, side), BF16), shape((8, 128), jnp.int32),
                   shape((blocks, 8, side), F32), scaled_t, send_t, send_t),
        in_specs=[spec(SMEM), spec(SMEM), spec(SMEM), spec(pltpu.HBM), spec(VMEM)],
        out_specs=(spec(VMEM), spec(SMEM), spec(VMEM), spec(VMEM), spec(VMEM), spec(VMEM)),
        scratch_shapes=[VMEM((blocks + 1, 8, side), F32), pltpu.SemaphoreType.DMA((16,))],
        compiler_params=params(41),
        name="setup",
    )(tile_index.T, tile_count, ghost_send[0], tile_values, start)

    vectors = [start]
    parts = []
    gram = None
    for level in range(1, STEPS + 1):
        last = level == STEPS
        got_b = lax.ppermute(send_b, AXIS, far)
        got_a = lax.ppermute(send_a, AXIS, near)
        args = [plan, tiles, scaled, got_a, vectors[-1]] + parts + ([gram] if gram is not None else [])
        acc, part, gram = pl.pallas_call(
            functools.partial(own_kernel, level - 1),
            out_shape=(acc_t, part_t, gram_t),
            in_specs=[spec(SMEM)] + [spec(VMEM)] * (len(args) - 1),
            out_specs=(spec(VMEM),) * 3,
            compiler_params=params(20),
            cost_estimate=pl.CostEstimate(flops=10**9, bytes_accessed=10**7, transcendentals=0),
            name="own",
        )(*args)
        parts.append(part)
        args = [plan, tiles, got_b, acc, scale]
        if level > 1:
            args.append(vectors[-2])
        if last:
            args += parts + [gram]
            outs = (part_t, gram_t, acc_t)
        else:
            outs = (vec_t, scaled_t, send_t, send_t, acc_t)
        got = pl.pallas_call(
            functools.partial(far_kernel, level, last),
            out_shape=outs,
            in_specs=[spec(SMEM)] + [spec(VMEM)] * (len(args) - 1),
            out_specs=(spec(VMEM),) * len(outs),
            input_output_aliases={3: len(outs) - 1},
            compiler_params=params(20),
            name="far",
        )(*args)
        if last:
            part, gram, _ = got
            parts.append(part)
        else:
            vec, scaled, send_a, send_b, _ = got
            vectors.append(vec)

    def phase(value, shift, count):
        mask = (count - 1) << shift
        moved = value
        for d in range(1, count):
            perm = [(i, (i & ~mask) | ((((i >> shift) + d) & (count - 1)) << shift)) for i in range(n)]
            moved = moved + lax.ppermute(value, AXIS, perm)
        return moved

    for shift, count in ((0, 2), (1, 4), (3, 4), (5, 4)):
        gram = phase(gram, shift, count)

    chunk = 1024
    basis_out, gram_matrix = pl.pallas_call(
        functools.partial(final_kernel, rows * n),
        out_shape=(shape((basis, rows), F32), shape((basis, basis), F32)),
        in_specs=[spec(VMEM)] * (STEPS + 2),
        out_specs=(spec(pltpu.HBM), spec(VMEM)),
        scratch_shapes=[VMEM((basis, 3 * basis), BF16), VMEM((rows // chunk, basis, chunk), F32),
                        pltpu.SemaphoreType.DMA((rows // chunk,))],
        compiler_params=params(20),
        name="final",
    )(gram, *parts)
    return basis_out.T, gram_matrix


def solution(mesh):
    placed = (
        P("parts", None),
        P("parts", None),
        P("parts", None, None),
        P("parts"),
        P("parts", None, None),
    )
    return jax.shard_map(
        body, mesh=mesh, in_specs=placed, out_specs=(P("parts", None), P()), check_vma=False
    )
```

```python
import functools

import jax
import jax.numpy as jnp
from jax import lax
from jax.experimental import pallas as pl
from jax.experimental.pallas import tpu as pltpu
from jax.sharding import PartitionSpec as P

STEPS = 4
AXIS = "parts"
VMEM = pltpu.VMEM
SMEM = pltpu.SMEM
F32 = jnp.float32
BF16 = jnp.bfloat16

SLOT, GROW, OCOL, OROW, SEND = range(5)


def spec(space):
    return pl.BlockSpec(memory_space=space)


def tile_product(block, tile):
    return lax.dot_general(block, tile, (((1,), (1,)), ((), ())), preferred_element_type=F32)


def quad_products(blocks, tiles):
    zero = jnp.zeros_like(blocks[0])
    join = jnp.concatenate
    out = []
    for i in range(0, len(blocks), 4):
        x, t = blocks[i:i + 4], tiles[i:i + 4]
        left = join([join([x[0], zero], 1), join([zero, x[1]], 1), join([x[2], zero], 1), join([zero, x[3]], 1)], 0)
        right = join([join([t[0], t[1]], 1), join([t[2], t[3]], 1)], 0)
        got = tile_product(left, right)
        out += [got[:16, :128], got[16:32, :128], got[32:48, 128:], got[48:, 128:]]
    return out


def spread_tiles(count, unroll, acc_ref, block_at, tile_at, row_at):
    def step(base, _):
        at = [base * unroll + u for u in range(unroll)]
        got = quad_products([block_at(t) for t in at], [tile_at(t) for t in at])
        for t, product in zip(at, got):
            acc_ref[row_at(t)] += product
        return 0

    lax.fori_loop(0, count // unroll, step, 0)


def pack(plan_ref, scaled_ref, send_a_ref, send_b_ref):
    half = send_a_ref.shape[0]

    def step(base, _):
        for u in range(8):
            g = base * 8 + u
            send_b_ref[g] = scaled_ref[plan_ref[SEND, half + g]]
        for u in range(8):
            g = base * 8 + u
            send_a_ref[g] = scaled_ref[plan_ref[SEND, g]]
        return 0

    lax.fori_loop(0, half // 8, step, 0)


def setup_kernel(index_in, ghost_in, values_ref, start_in, count_ref,
                 tiles_ref, plan_ref, scale_ref, scaled_ref, send_a_ref, send_b_ref,
                 acc_ref, index_ref, ghost_ref, start_ref, sems):
    total, side = values_ref.shape[0], values_ref.shape[1]
    blocks = scaled_ref.shape[0]
    half = send_a_ref.shape[0]
    ghosts = 2 * half
    chunks = sems.shape[0] - 3
    per = total // chunks

    def copy(k):
        return pltpu.make_async_copy(
            values_ref.at[pl.ds(k * per, per)], tiles_ref.at[pl.ds(k * per, per)], sems.at[k]
        )

    small = [pltpu.make_async_copy(a, b, sems.at[chunks + i]) for i, (a, b) in enumerate(
        ((index_in, index_ref), (ghost_in, ghost_ref), (start_in, start_ref)))]
    for c in small[:2]:
        c.start()
    for k in range(chunks):
        copy(k).start()
    small[2].start()
    for c in small[:2]:
        c.wait()

    odd = lax.rem(lax.axis_index(AXIS), 2)
    flip = (1 - odd) * half
    count = count_ref[0]
    acc_ref[...] = jnp.zeros_like(acc_ref)

    def ghost_plan(base, _):
        for u in range(4):
            t = base * 4 + u
            place = jnp.bitwise_xor(index_ref[1, t] - blocks, flip)
            plan_ref[SLOT, place] = t
            plan_ref[GROW, place] = index_ref[0, t]
            plan_ref[OCOL, t] = index_ref[1, ghosts + t]
            plan_ref[OROW, t] = jnp.where(ghosts + t < count, index_ref[0, ghosts + t], blocks)
        return 0

    lax.fori_loop(0, ghosts // 4, ghost_plan, 0)

    def send_plan(g, _):
        plan_ref[SEND, g] = ghost_ref[odd, g]
        plan_ref[SEND, half + g] = ghost_ref[1 - odd, g]
        return 0

    lax.fori_loop(0, half, send_plan, 0)

    row = lax.broadcasted_iota(jnp.int32, (16, 2 * side), 0)
    lane = lax.broadcasted_iota(jnp.int32, (16, 2 * side), 1)
    ones = jnp.where((row < 8) == (lane < side), 1.0, 0.0).astype(BF16)
    join = jnp.concatenate
    for k in range(chunks):
        copy(k).wait()
        slots = [k * per + u for u in range(per)]
        got = []
        for i in range(0, per, 4):
            t = [tiles_ref[slot] for slot in slots[i:i + 4]]
            sums = tile_product(ones, join([join([t[0], t[1]], 1), join([t[2], t[3]], 1)], 0))
            got += [sums[:8, :side], sums[8:, :side], sums[:8, side:], sums[8:, side:]]
        for t, part in zip(slots, got):
            target = index_ref[0, t]
            if t >= ghosts:
                target = jnp.where(t < count, target, blocks)
            acc_ref[target] += part

    small[2].wait()

    def scale_step(base, _):
        for u in range(8):
            b = base * 8 + u
            factor = lax.rsqrt(1.0 + acc_ref[b])
            scale_ref[b] = factor
            at = pl.ds(pl.multiple_of(b * side, side), side)
            scaled_ref[b] = (join([factor, factor], 0) * start_ref[:, at]).astype(BF16)
        return 0

    lax.fori_loop(0, blocks // 8, scale_step, 0)
    pack(plan_ref, scaled_ref, send_a_ref, send_b_ref)


def split(value):
    high = value.astype(BF16)
    return high, (value - high.astype(F32)).astype(BF16)


def gram_rows(parts, gram_ref, level):
    rows = parts[0].shape[1]
    chunk = 1024
    width = 16 * (level + 1)
    acc = jnp.zeros((32, 2 * width), F32)
    for k in range(rows // chunk):
        at = slice(k * chunk, (k + 1) * chunk)
        right = jnp.concatenate([p[:16, at] for p in parts] + [p[16:, at] for p in parts], 0)
        acc += lax.dot_general(parts[-1][:, at], right, (((1,), (1,)), ((), ())), preferred_element_type=F32)
    both = acc[:16] + acc[16:]
    gram_ref[16 * level:16 * (level + 1), :width] = both[:, :width] + both[:, width:]


def own_kernel(level, *refs):
    plan_ref, tiles_ref, scaled_ref, got_ref, vec_ref = refs[:5]
    older = refs[5:5 + level]
    at = 5 + level
    gram_in = None
    if level:
        gram_in = refs[at]
        at += 1
    acc_ref, part_ref, gram_ref = refs[at:at + 3]
    half = got_ref.shape[0]
    acc_ref[...] = jnp.zeros_like(acc_ref)
    ghosts = 2 * half

    spread_tiles(ghosts, 32, acc_ref, lambda t: scaled_ref[plan_ref[OCOL, t]],
                 lambda t: tiles_ref[ghosts + t], lambda t: plan_ref[OROW, t])
    spread_tiles(half, 32, acc_ref, lambda g: got_ref[g],
                 lambda g: tiles_ref[plan_ref[SLOT, g]], lambda g: plan_ref[GROW, g])
    high, low = split(vec_ref[...])
    part_ref[:16] = high
    part_ref[16:] = low
    gram_ref[...] = gram_in[...] if level else jnp.zeros_like(gram_ref)
    gram_rows(tuple(older) + (part_ref,), gram_ref, level)


def far_kernel(level, last, *refs):
    plan_ref, tiles_ref, got_ref, _, scale_ref = refs[:5]
    at = 5
    prev_ref = None
    if level > 1:
        prev_ref = refs[at]
        at += 1
    if last:
        older = refs[at:at + level]
        gram_in = refs[at + level]
        at += level + 1
        part_ref, gram_ref, acc_ref = refs[at:at + 3]
    else:
        vec_ref, scaled_ref, send_a_ref, send_b_ref, acc_ref = refs[at:at + 5]
    half = got_ref.shape[0]
    side = tiles_ref.shape[1]
    blocks = scale_ref.shape[0]
    spread_tiles(half, 32, acc_ref, lambda g: got_ref[g],
                 lambda g: tiles_ref[plan_ref[SLOT, half + g]], lambda g: plan_ref[GROW, half + g])

    def close_step(base, _):
        for u in range(8):
            b = base * 8 + u
            where = pl.ds(pl.multiple_of(b * side, side), side)
            factor = jnp.concatenate([scale_ref[b], scale_ref[b]], 0)
            value = factor * acc_ref[b]
            if level > 1:
                value = 2.0 * value - prev_ref[:, where]
            if last:
                high, low = split(value)
                part_ref[:16, where] = high
                part_ref[16:, where] = low
            else:
                vec_ref[:, where] = value
                scaled_ref[b] = (factor * value).astype(BF16)
        return 0

    lax.fori_loop(0, blocks // 8, close_step, 0)
    if last:
        gram_ref[...] = gram_in[...]
        gram_rows(tuple(older) + (part_ref,), gram_ref, level)
    else:
        pack(plan_ref, scaled_ref, send_a_ref, send_b_ref)


def inverse_factor(gram):
    groups = gram.shape[0] // 8
    full = (8, 128)
    row8 = lax.broadcasted_iota(jnp.int32, full, 0)
    lane = lax.broadcasted_iota(jnp.int32, full, 1)
    left = [gram[8 * g:8 * g + 8] for g in range(groups)]
    right = [jnp.where(lane == row8 + 8 * g, 1.0, 0.0) for g in range(groups)]

    def across(value, at):
        return jnp.broadcast_to(value[:, at:at + 1], full)

    def down(value, at):
        return jnp.broadcast_to(value[at:at + 1, :], full)

    def column(entries):
        out = jnp.zeros(full, F32)
        for i, entry in entries:
            out = jnp.where(row8 == i, entry, out)
        return out

    def combine(columns, value):
        return sum(c * down(value, k) for k, c in enumerate(columns))

    done = []
    for p in range(groups):
        a, b = left[p], right[p]
        spread = [across(a, 8 * p + k) for k in range(8)]
        e = [[down(spread[k], i) for k in range(i + 1)] for i in range(8)]
        scale = []
        for k in range(8):
            scale.append(lax.rsqrt(e[k][k]))
            for i in range(k + 1, 8):
                e[i][k] = e[i][k] * scale[k]
            for i in range(k + 1, 8):
                for j in range(k + 1, i + 1):
                    e[i][j] = e[i][j] - e[i][k] * e[j][k]
        m = [[None] * 8 for _ in range(8)]
        for j in range(8):
            m[j][j] = scale[j]
            for i in range(j + 1, 8):
                m[i][j] = -scale[i] * sum(e[i][k] * m[k][j] for k in range(j, i))
        solve = [column([(i, m[i][k]) for i in range(k, 8)]) for k in range(8)]
        ua, ub = combine(solve, a), combine(solve, b)
        done.append(ub)
        if p + 1 < groups:
            back = [column([(k, m[i][k]) for k in range(i + 1)]) for i in range(8)]
            wa, wb = combine(back, ua), combine(back, ub)
            wa, wb = [down(wa, k) for k in range(8)], [down(wb, k) for k in range(8)]
            for g in range(p + 1, groups):
                factors = [across(left[g], 8 * p + k) for k in range(8)]
                left[g] = left[g] - sum(f * w for f, w in zip(factors, wa))
                right[g] = right[g] - sum(f * w for f, w in zip(factors, wb))
    return jnp.concatenate(done, 0)


def final_kernel(row_total, gram_in, *refs):
    parts = refs[:STEPS + 1]
    basis_ref, gram_ref, mix_ref, stage_ref, sems = refs[STEPS + 1:]
    width = gram_ref.shape[0]

    if True:
        lower = gram_in[...] * (1.0 / row_total)
        row = lax.broadcasted_iota(jnp.int32, lower.shape, 0)
        lane = lax.broadcasted_iota(jnp.int32, lower.shape, 1)
        lower = jnp.where(row >= lane, lower, 0.0)
        strict = jnp.where(row > lane, lower, 0.0)
        square = jnp.concatenate([strict, jnp.zeros((128 - width, 128), F32)], 0)
        full = lower + square.T[:width]
        gram_ref[...] = full[:, :width]
        inverse = inverse_factor(full)
        high, low = split(inverse[:, :width])
        mix_ref[...] = jnp.concatenate([high, low, high], 1)

    pieces = stage_ref.shape[0]
    chunk = stage_ref.shape[2]

    def out(k):
        return pltpu.make_async_copy(stage_ref.at[k], basis_ref.at[:, pl.ds(k * chunk, chunk)], sems.at[k])

    mix = mix_ref[...]
    for k in range(pieces):
        at = slice(k * chunk, (k + 1) * chunk)
        tops = [p[:16, at] for p in parts]
        lows = [p[16:, at] for p in parts]
        stack = jnp.concatenate(tops + tops + lows, 0)
        stage_ref[k] = jnp.dot(mix, stack, preferred_element_type=F32)
        out(k).start()
    for k in range(pieces):
        out(k).wait()


def params(mib, **kw):
    return pltpu.CompilerParams(vmem_limit_bytes=mib * 2**20, **kw)


def body(start_vectors, tile_index, tile_values, tile_count, ghost_send):
    rows, width = start_vectors.shape
    total, side, _ = tile_values.shape
    blocks = rows // side
    half = ghost_send.shape[2]
    n = lax.axis_size(AXIS)
    basis = width * (STEPS + 1)
    shape = jax.ShapeDtypeStruct

    scaled_t = shape((blocks, width, side), BF16)
    send_t = shape((half, width, side), BF16)
    vec_t = shape((width, rows), F32)
    part_t = shape((2 * width, rows), BF16)
    acc_t = shape((blocks + 1, width, side), F32)
    gram_t = shape((basis, 128), F32)

    near = [(i, i ^ 1) for i in range(n)]
    far = [(i, (i + 1) % n if i % 2 else (i - 1) % n) for i in range(n)]

    start = start_vectors.T
    tiles, plan, scale, scaled, send_a, send_b = pl.pallas_call(
        setup_kernel,
        out_shape=(shape((total, side, side), BF16), shape((8, 128), jnp.int32),
                   shape((blocks, 8, side), F32), scaled_t, send_t, send_t),
        in_specs=[spec(pltpu.HBM)] * 4 + [spec(SMEM)],
        out_specs=(spec(VMEM), spec(SMEM), spec(VMEM), spec(VMEM), spec(VMEM), spec(VMEM)),
        scratch_shapes=[VMEM((blocks + 1, 8, side), F32), SMEM((2, total), jnp.int32),
                        SMEM((2, half), jnp.int32), VMEM((width, rows), F32), pltpu.SemaphoreType.DMA((4 + 3,))],
        compiler_params=params(41),
        name="setup",
    )(*[pltpu.with_memory_space_constraint(v, pltpu.HBM)
        for v in (tile_index.T, ghost_send[0], tile_values, start)], tile_count)

    vectors = [start]
    parts = []
    gram = None
    for level in range(1, STEPS + 1):
        last = level == STEPS
        got_b = lax.ppermute(send_b, AXIS, far)
        got_a = lax.ppermute(send_a, AXIS, near)
        args = [plan, tiles, scaled, got_a, vectors[-1]] + parts + ([gram] if gram is not None else [])
        acc, part, gram = pl.pallas_call(
            functools.partial(own_kernel, level - 1),
            out_shape=(acc_t, part_t, gram_t),
            in_specs=[spec(SMEM)] + [spec(VMEM)] * (len(args) - 1),
            out_specs=(spec(VMEM),) * 3,
            compiler_params=params(20),
            cost_estimate=pl.CostEstimate(flops=10**9, bytes_accessed=10**7, transcendentals=0),
            name="own",
        )(*args)
        parts.append(part)
        args = [plan, tiles, got_b, acc, scale]
        if level > 1:
            args.append(vectors[-2])
        if last:
            args += parts + [gram]
            outs = (part_t, gram_t, acc_t)
        else:
            outs = (vec_t, scaled_t, send_t, send_t, acc_t)
        got = pl.pallas_call(
            functools.partial(far_kernel, level, last),
            out_shape=outs,
            in_specs=[spec(SMEM)] + [spec(VMEM)] * (len(args) - 1),
            out_specs=(spec(VMEM),) * len(outs),
            input_output_aliases={3: len(outs) - 1},
            compiler_params=params(20),
            name="far",
        )(*args)
        if last:
            part, gram, _ = got
            parts.append(part)
        else:
            vec, scaled, send_a, send_b, _ = got
            vectors.append(vec)

    def phase(value, shift, count):
        mask = (count - 1) << shift
        moved = value
        for d in range(1, count):
            perm = [(i, (i & ~mask) | ((((i >> shift) + d) & (count - 1)) << shift)) for i in range(n)]
            moved = moved + lax.ppermute(value, AXIS, perm)
        return moved

    for shift, count in ((0, 2), (1, 4), (3, 4), (5, 4)):
        gram = phase(gram, shift, count)

    chunk = 1024
    basis_out, gram_matrix = pl.pallas_call(
        functools.partial(final_kernel, rows * n),
        out_shape=(shape((basis, rows), F32), shape((basis, basis), F32)),
        in_specs=[spec(VMEM)] * (STEPS + 2),
        out_specs=(spec(pltpu.HBM), spec(VMEM)),
        scratch_shapes=[VMEM((basis, 3 * basis), BF16), VMEM((rows // chunk, basis, chunk), F32),
                        pltpu.SemaphoreType.DMA((rows // chunk,))],
        compiler_params=params(20),
        name="final",
    )(gram, *parts)
    return basis_out.T, gram_matrix


def solution(mesh):
    placed = (
        P("parts", None),
        P("parts", None),
        P("parts", None, None),
        P("parts"),
        P("parts", None, None),
    )
    return jax.shard_map(
        body, mesh=mesh, in_specs=placed, out_specs=(P("parts", None), P()), check_vma=False
    )
```

```python
import functools

import jax
import jax.numpy as jnp
from jax import lax
from jax.experimental import pallas as pl
from jax.experimental.pallas import tpu as pltpu
from jax.sharding import PartitionSpec as P

STEPS = 4
AXIS = "parts"
VMEM = pltpu.VMEM
SMEM = pltpu.SMEM
F32 = jnp.float32
BF16 = jnp.bfloat16

SLOT, GROW, OCOL, OROW, SEND = range(5)
LIST = 128


def spec(space):
    return pl.BlockSpec(memory_space=space)


def tile_product(block, tile):
    return lax.dot_general(block, tile, (((1,), (1,)), ((), ())), preferred_element_type=F32)


def quad_products(blocks, tiles):
    zero = jnp.zeros_like(blocks[0])
    join = jnp.concatenate
    out = []
    for i in range(0, len(blocks), 4):
        x, t = blocks[i:i + 4], tiles[i:i + 4]
        left = join([join([x[0], zero], 1), join([zero, x[1]], 1), join([x[2], zero], 1), join([zero, x[3]], 1)], 0)
        right = join([join([t[0], t[1]], 1), join([t[2], t[3]], 1)], 0)
        got = tile_product(left, right)
        out += [got[:16, :128], got[16:32, :128], got[32:48, 128:], got[48:, 128:]]
    return out


def spread_tiles(count, unroll, acc_ref, block_at, tile_at, row_at):
    def step(base, _):
        at = [base * unroll + u for u in range(unroll)]
        got = quad_products([block_at(t) for t in at], [tile_at(t) for t in at])
        for t, product in zip(at, got):
            acc_ref[row_at(t)] += product
        return 0

    lax.fori_loop(0, count // unroll, step, 0)


def pack(plan_ref, scaled_ref, send_a_ref, send_b_ref):
    half = send_a_ref.shape[0]

    def step(base, _):
        for u in range(8):
            g = base * 8 + u
            send_b_ref[g] = scaled_ref[plan_ref[SEND * LIST + half + g]]
        for u in range(8):
            g = base * 8 + u
            send_a_ref[g] = scaled_ref[plan_ref[SEND * LIST + g]]
        return 0

    lax.fori_loop(0, half // 8, step, 0)


def setup_kernel(index_in, ghost_in, values_ref, start_in, count_ref,
                 tiles_ref, plan_ref, scale_ref, scaled_ref, send_a_ref, send_b_ref,
                 acc_ref, index_ref, ghost_ref, start_ref, sems):
    total, side = values_ref.shape[0], values_ref.shape[1]
    blocks = scaled_ref.shape[0]
    half = send_a_ref.shape[0]
    ghosts = 2 * half
    chunks = sems.shape[0] - 3
    per = total // chunks

    def copy(k):
        return pltpu.make_async_copy(
            values_ref.at[pl.ds(k * per, per)], tiles_ref.at[pl.ds(k * per, per)], sems.at[k]
        )

    small = [pltpu.make_async_copy(a, b, sems.at[chunks + i]) for i, (a, b) in enumerate(
        ((index_in, index_ref), (ghost_in, ghost_ref), (start_in, start_ref)))]
    for c in small[:2]:
        c.start()
    for k in range(chunks):
        copy(k).start()
    small[2].start()
    for c in small[:2]:
        c.wait()

    odd = lax.rem(lax.axis_index(AXIS), 2)
    flip = (1 - odd) * half
    count = count_ref[0]
    acc_ref[...] = jnp.zeros_like(acc_ref)

    def ghost_plan(base, _):
        for u in range(4):
            t = base * 4 + u
            place = jnp.bitwise_xor(index_ref[1, t] - blocks, flip)
            plan_ref[SLOT * LIST + place] = t
            plan_ref[GROW * LIST + place] = index_ref[0, t]
            plan_ref[OCOL * LIST + t] = index_ref[1, ghosts + t]
            plan_ref[OROW * LIST + t] = jnp.where(ghosts + t < count, index_ref[0, ghosts + t], blocks)
        return 0

    lax.fori_loop(0, ghosts // 4, ghost_plan, 0)

    def send_plan(g, _):
        plan_ref[SEND * LIST + g] = ghost_ref[odd, g]
        plan_ref[SEND * LIST + half + g] = ghost_ref[1 - odd, g]
        return 0

    lax.fori_loop(0, half, send_plan, 0)

    row = lax.broadcasted_iota(jnp.int32, (16, 2 * side), 0)
    lane = lax.broadcasted_iota(jnp.int32, (16, 2 * side), 1)
    ones = jnp.where((row < 8) == (lane < side), 1.0, 0.0).astype(BF16)
    join = jnp.concatenate
    for k in range(chunks):
        copy(k).wait()
        slots = [k * per + u for u in range(per)]
        got = []
        for i in range(0, per, 4):
            t = [tiles_ref[slot] for slot in slots[i:i + 4]]
            sums = tile_product(ones, join([join([t[0], t[1]], 1), join([t[2], t[3]], 1)], 0))
            got += [sums[:8, :side], sums[8:, :side], sums[:8, side:], sums[8:, side:]]
        for t, part in zip(slots, got):
            target = index_ref[0, t]
            if t >= ghosts:
                target = jnp.where(t < count, target, blocks)
            acc_ref[target] += part

    small[2].wait()

    def scale_step(base, _):
        for u in range(8):
            b = base * 8 + u
            factor = lax.rsqrt(1.0 + acc_ref[b])
            scale_ref[b] = factor
            at = pl.ds(pl.multiple_of(b * side, side), side)
            scaled_ref[b] = (join([factor, factor], 0) * start_ref[:, at]).astype(BF16)
        return 0

    lax.fori_loop(0, blocks // 8, scale_step, 0)
    pack(plan_ref, scaled_ref, send_a_ref, send_b_ref)


def split(value):
    high = value.astype(BF16)
    return high, (value - high.astype(F32)).astype(BF16)


def gram_rows(parts, gram_ref, level):
    rows = parts[0].shape[1]
    chunk = 1024
    width = 16 * (level + 1)
    acc = jnp.zeros((2 * width, 32), F32)
    for k in range(rows // chunk):
        at = slice(k * chunk, (k + 1) * chunk)
        right = jnp.concatenate([p[:16, at] for p in parts] + [p[16:, at] for p in parts], 0)
        acc += lax.dot_general(right, parts[-1][:, at], (((1,), (1,)), ((), ())), preferred_element_type=F32)
    acc = jnp.concatenate([acc, jnp.zeros((2 * width, 96), F32)], 1)
    if 2 * width % 128:
        acc = jnp.concatenate([acc, jnp.zeros(((-2 * width) % 128, 128), F32)], 0)
    acc = acc.T
    both = acc[:16] + acc[16:32]
    gram_ref[16 * level:16 * (level + 1), :width] = both[:, :width] + both[:, width:2 * width]


def own_kernel(level, *refs):
    plan_ref, tiles_ref, scaled_ref, got_ref, vec_ref = refs[:5]
    older = refs[5:5 + level]
    at = 5 + level
    gram_in = None
    if level:
        gram_in = refs[at]
        at += 1
    acc_ref, part_ref, gram_ref = refs[at:at + 3]
    half = got_ref.shape[0]
    acc_ref[...] = jnp.zeros_like(acc_ref)
    ghosts = 2 * half

    spread_tiles(ghosts, 32, acc_ref, lambda t: scaled_ref[plan_ref[OCOL * LIST + t]],
                 lambda t: tiles_ref[ghosts + t], lambda t: plan_ref[OROW * LIST + t])
    spread_tiles(half, 32, acc_ref, lambda g: got_ref[g],
                 lambda g: tiles_ref[plan_ref[SLOT * LIST + g]], lambda g: plan_ref[GROW * LIST + g])
    high, low = split(vec_ref[...])
    part_ref[:16] = high
    part_ref[16:] = low
    gram_ref[...] = gram_in[...] if level else jnp.zeros_like(gram_ref)
    gram_rows(tuple(older) + (part_ref,), gram_ref, level)


def far_kernel(level, last, *refs):
    plan_ref, tiles_ref, got_ref, _, scale_ref = refs[:5]
    at = 5
    prev_ref = None
    if level > 1:
        prev_ref = refs[at]
        at += 1
    if last:
        older = refs[at:at + level]
        gram_in = refs[at + level]
        at += level + 1
        part_ref, gram_ref, acc_ref = refs[at:at + 3]
    else:
        vec_ref, scaled_ref, send_a_ref, send_b_ref, acc_ref = refs[at:at + 5]
    half = got_ref.shape[0]
    side = tiles_ref.shape[1]
    blocks = scale_ref.shape[0]
    spread_tiles(half, 32, acc_ref, lambda g: got_ref[g],
                 lambda g: tiles_ref[plan_ref[SLOT * LIST + half + g]], lambda g: plan_ref[GROW * LIST + half + g])

    def close_step(base, _):
        for u in range(8):
            b = base * 8 + u
            where = pl.ds(pl.multiple_of(b * side, side), side)
            factor = jnp.concatenate([scale_ref[b], scale_ref[b]], 0)
            value = factor * acc_ref[b]
            if level > 1:
                value = 2.0 * value - prev_ref[:, where]
            if last:
                high, low = split(value)
                part_ref[:16, where] = high
                part_ref[16:, where] = low
            else:
                vec_ref[:, where] = value
                scaled_ref[b] = (factor * value).astype(BF16)
        return 0

    lax.fori_loop(0, blocks // 8, close_step, 0)
    if last:
        gram_ref[...] = gram_in[...]
        gram_rows(tuple(older) + (part_ref,), gram_ref, level)
    else:
        pack(plan_ref, scaled_ref, send_a_ref, send_b_ref)


def inverse_factor(gram):
    groups = gram.shape[0] // 8
    full = (8, 128)
    row8 = lax.broadcasted_iota(jnp.int32, full, 0)
    lane = lax.broadcasted_iota(jnp.int32, full, 1)
    left = [gram[8 * g:8 * g + 8] for g in range(groups)]
    right = [jnp.where(lane == row8 + 8 * g, 1.0, 0.0) for g in range(groups)]

    def across(value, at):
        return jnp.broadcast_to(value[:, at:at + 1], full)

    def down(value, at):
        return jnp.broadcast_to(value[at:at + 1, :], full)

    def column(entries):
        out = jnp.zeros(full, F32)
        for i, entry in entries:
            out = jnp.where(row8 == i, entry, out)
        return out

    def combine(columns, value):
        return sum(c * down(value, k) for k, c in enumerate(columns))

    done = []
    for p in range(groups):
        a, b = left[p], right[p]
        spread = [across(a, 8 * p + k) for k in range(8)]
        e = [[down(spread[k], i) for k in range(i + 1)] for i in range(8)]
        scale = []
        for k in range(8):
            scale.append(lax.rsqrt(e[k][k]))
            for i in range(k + 1, 8):
                e[i][k] = e[i][k] * scale[k]
            for i in range(k + 1, 8):
                for j in range(k + 1, i + 1):
                    e[i][j] = e[i][j] - e[i][k] * e[j][k]
        m = [[None] * 8 for _ in range(8)]
        for j in range(8):
            m[j][j] = scale[j]
            for i in range(j + 1, 8):
                m[i][j] = -scale[i] * sum(e[i][k] * m[k][j] for k in range(j, i))
        solve = [column([(i, m[i][k]) for i in range(k, 8)]) for k in range(8)]
        ua, ub = combine(solve, a), combine(solve, b)
        done.append(ub)
        if p + 1 < groups:
            back = [column([(k, m[i][k]) for k in range(i + 1)]) for i in range(8)]
            wa, wb = combine(back, ua), combine(back, ub)
            wa, wb = [down(wa, k) for k in range(8)], [down(wb, k) for k in range(8)]
            for g in range(p + 1, groups):
                factors = [across(left[g], 8 * p + k) for k in range(8)]
                left[g] = left[g] - sum(f * w for f, w in zip(factors, wa))
                right[g] = right[g] - sum(f * w for f, w in zip(factors, wb))
    return jnp.concatenate(done, 0)


def final_kernel(row_total, gram_in, *refs):
    parts = refs[:STEPS + 1]
    basis_ref, gram_ref, mix_ref, stage_ref, sems = refs[STEPS + 1:]
    width = gram_ref.shape[0]

    if True:
        lower = gram_in[...] * (1.0 / row_total)
        row = lax.broadcasted_iota(jnp.int32, lower.shape, 0)
        lane = lax.broadcasted_iota(jnp.int32, lower.shape, 1)
        lower = jnp.where(row >= lane, lower, 0.0)
        strict = jnp.where(row > lane, lower, 0.0)
        square = jnp.concatenate([strict, jnp.zeros((128 - width, 128), F32)], 0)
        full = lower + square.T[:width]
        gram_ref[...] = full[:, :width]
        inverse = inverse_factor(full)
        high, low = split(inverse[:, :width])
        mix_ref[...] = jnp.concatenate([high, low, high], 1)

    pieces = stage_ref.shape[0]
    chunk = stage_ref.shape[2]

    def out(k):
        return pltpu.make_async_copy(stage_ref.at[k], basis_ref.at[:, pl.ds(k * chunk, chunk)], sems.at[k])

    mix = mix_ref[...]
    for k in range(pieces):
        at = slice(k * chunk, (k + 1) * chunk)
        tops = [p[:16, at] for p in parts]
        lows = [p[16:, at] for p in parts]
        stack = jnp.concatenate(tops + tops + lows, 0)
        stage_ref[k] = jnp.dot(mix, stack, preferred_element_type=F32)
        out(k).start()
    for k in range(pieces):
        out(k).wait()


def params(mib, **kw):
    return pltpu.CompilerParams(vmem_limit_bytes=mib * 2**20, **kw)


def body(start_vectors, tile_index, tile_values, tile_count, ghost_send):
    rows, width = start_vectors.shape
    total, side, _ = tile_values.shape
    blocks = rows // side
    half = ghost_send.shape[2]
    n = lax.axis_size(AXIS)
    basis = width * (STEPS + 1)
    shape = jax.ShapeDtypeStruct

    scaled_t = shape((blocks, width, side), BF16)
    send_t = shape((half, width, side), BF16)
    vec_t = shape((width, rows), F32)
    part_t = shape((2 * width, rows), BF16)
    acc_t = shape((blocks + 1, width, side), F32)
    gram_t = shape((basis, 128), F32)

    near = [(i, i ^ 1) for i in range(n)]
    far = [(i, (i + 1) % n if i % 2 else (i - 1) % n) for i in range(n)]

    start = start_vectors.T
    tiles, plan, scale, scaled, send_a, send_b = pl.pallas_call(
        setup_kernel,
        out_shape=(shape((total, side, side), BF16), SMEM((5 * LIST,), jnp.int32),
                   shape((blocks, 8, side), F32), scaled_t, send_t, send_t),
        in_specs=[spec(pltpu.HBM)] * 4 + [spec(SMEM)],
        out_specs=(spec(VMEM), spec(SMEM), spec(VMEM), spec(VMEM), spec(VMEM), spec(VMEM)),
        scratch_shapes=[VMEM((blocks + 1, 8, side), F32), SMEM((2, total), jnp.int32),
                        SMEM((2, half), jnp.int32), VMEM((width, rows), F32), pltpu.SemaphoreType.DMA((4 + 3,))],
        compiler_params=params(41),
        name="setup",
    )(*[pltpu.with_memory_space_constraint(v, pltpu.HBM)
        for v in (tile_index.T, ghost_send[0], tile_values, start)], tile_count)

    vectors = [start]
    parts = []
    gram = None
    for level in range(1, STEPS + 1):
        last = level == STEPS
        got_b = lax.ppermute(send_b, AXIS, far)
        got_a = lax.ppermute(send_a, AXIS, near)
        args = [plan, tiles, scaled, got_a, vectors[-1]] + parts + ([gram] if gram is not None else [])
        acc, part, gram = pl.pallas_call(
            functools.partial(own_kernel, level - 1),
            out_shape=(acc_t, part_t, gram_t),
            in_specs=[spec(SMEM)] + [spec(VMEM)] * (len(args) - 1),
            out_specs=(spec(VMEM),) * 3,
            compiler_params=params(20),
            cost_estimate=pl.CostEstimate(flops=10**9, bytes_accessed=10**7, transcendentals=0),
            name="own",
        )(*args)
        parts.append(part)
        args = [plan, tiles, got_b, acc, scale]
        if level > 1:
            args.append(vectors[-2])
        if last:
            args += parts + [gram]
            outs = (part_t, gram_t, acc_t)
        else:
            outs = (vec_t, scaled_t, send_t, send_t, acc_t)
        got = pl.pallas_call(
            functools.partial(far_kernel, level, last),
            out_shape=outs,
            in_specs=[spec(SMEM)] + [spec(VMEM)] * (len(args) - 1),
            out_specs=(spec(VMEM),) * len(outs),
            input_output_aliases={3: len(outs) - 1},
            compiler_params=params(20),
            name="far",
        )(*args)
        if last:
            part, gram, _ = got
            parts.append(part)
        else:
            vec, scaled, send_a, send_b, _ = got
            vectors.append(vec)

    def phase(value, shift, count):
        mask = (count - 1) << shift
        moved = value
        for d in range(1, count):
            perm = [(i, (i & ~mask) | ((((i >> shift) + d) & (count - 1)) << shift)) for i in range(n)]
            moved = moved + lax.ppermute(value, AXIS, perm)
        return moved

    for shift, count in ((0, 2), (1, 4), (3, 4), (5, 4)):
        gram = phase(gram, shift, count)

    chunk = 1024
    basis_out, gram_matrix = pl.pallas_call(
        functools.partial(final_kernel, rows * n),
        out_shape=(shape((basis, rows), F32), shape((basis, basis), F32)),
        in_specs=[spec(VMEM)] * (STEPS + 2),
        out_specs=(spec(pltpu.HBM), spec(VMEM)),
        scratch_shapes=[VMEM((basis, 3 * basis), BF16), VMEM((rows // chunk, basis, chunk), F32),
                        pltpu.SemaphoreType.DMA((rows // chunk,))],
        compiler_params=params(20),
        name="final",
    )(gram, *parts)
    return basis_out.T, gram_matrix


def solution(mesh):
    placed = (
        P("parts", None),
        P("parts", None),
        P("parts", None, None),
        P("parts"),
        P("parts", None, None),
    )
    return jax.shard_map(
        body, mesh=mesh, in_specs=placed, out_specs=(P("parts", None), P()), check_vma=False
    )
```

```python
import functools

import jax
import jax.numpy as jnp
from jax import lax
from jax.experimental import pallas as pl
from jax.experimental.pallas import tpu as pltpu
from jax.sharding import PartitionSpec as P

STEPS = 4
AXIS = "parts"
VMEM = pltpu.VMEM
SMEM = pltpu.SMEM
F32 = jnp.float32
BF16 = jnp.bfloat16

SLOT, GROW, OCOL, OROW, SEND = range(5)
LIST = 128
CHUNKS = (0, 128, 256)


def spec(space):
    return pl.BlockSpec(memory_space=space)


def tile_product(block, tile):
    return lax.dot_general(block, tile, (((1,), (1,)), ((), ())), preferred_element_type=F32)


def quad_products(blocks, tiles):
    zero = jnp.zeros_like(blocks[0])
    join = jnp.concatenate
    out = []
    for i in range(0, len(blocks), 4):
        x, t = blocks[i:i + 4], tiles[i:i + 4]
        left = join([join([x[0], zero], 1), join([zero, x[1]], 1), join([x[2], zero], 1), join([zero, x[3]], 1)], 0)
        right = join([join([t[0], t[1]], 1), join([t[2], t[3]], 1)], 0)
        got = tile_product(left, right)
        out += [got[:16, :128], got[16:32, :128], got[32:48, 128:], got[48:, 128:]]
    return out


def spread_tiles(count, unroll, acc_ref, block_at, tile_at, row_at):
    def step(base, _):
        at = [base * unroll + u for u in range(unroll)]
        got = quad_products([block_at(t) for t in at], [tile_at(t) for t in at])
        for t, product in zip(at, got):
            acc_ref[row_at(t)] += product
        return 0

    lax.fori_loop(0, count // unroll, step, 0)


def pack(plan_ref, scaled_ref, send_a_ref, send_b_ref):
    half = send_a_ref.shape[0]

    def step(base, _):
        for u in range(8):
            g = base * 8 + u
            send_b_ref[g] = scaled_ref[plan_ref[SEND * LIST + half + g]]
        for u in range(8):
            g = base * 8 + u
            send_a_ref[g] = scaled_ref[plan_ref[SEND * LIST + g]]
        return 0

    lax.fori_loop(0, half // 8, step, 0)


def setup_kernel(index_in, ghost_in, values_ref, start_in, count_ref,
                 tiles_ref, plan_ref, scale_ref, scaled_ref, send_a_ref, send_b_ref,
                 acc_ref, index_ref, ghost_ref, start_ref, sems):
    total, side = values_ref.shape[0], values_ref.shape[1]
    blocks = scaled_ref.shape[0]
    half = send_a_ref.shape[0]
    ghosts = 2 * half
    chunks = len(CHUNKS) - 1

    def copy(k):
        at = pl.ds(CHUNKS[k], CHUNKS[k + 1] - CHUNKS[k])
        return pltpu.make_async_copy(values_ref.at[at], tiles_ref.at[at], sems.at[k])

    small = [pltpu.make_async_copy(a, b, sems.at[chunks + i]) for i, (a, b) in enumerate(
        ((index_in, index_ref), (ghost_in, ghost_ref), (start_in, start_ref)))]
    for c in small[:2]:
        c.start()
    for k in range(chunks):
        copy(k).start()
    small[2].start()
    for c in small[:2]:
        c.wait()

    odd = lax.rem(lax.axis_index(AXIS), 2)
    flip = (1 - odd) * half
    count = count_ref[0]
    acc_ref[...] = jnp.zeros_like(acc_ref)

    def ghost_plan(base, _):
        for u in range(4):
            t = base * 4 + u
            place = jnp.bitwise_xor(index_ref[1, t] - blocks, flip)
            plan_ref[SLOT * LIST + place] = t
            plan_ref[GROW * LIST + place] = index_ref[0, t]
            plan_ref[OCOL * LIST + t] = index_ref[1, ghosts + t]
            plan_ref[OROW * LIST + t] = jnp.where(ghosts + t < count, index_ref[0, ghosts + t], blocks)
        return 0

    lax.fori_loop(0, ghosts // 4, ghost_plan, 0)

    def send_plan(g, _):
        plan_ref[SEND * LIST + g] = ghost_ref[odd, g]
        plan_ref[SEND * LIST + half + g] = ghost_ref[1 - odd, g]
        return 0

    lax.fori_loop(0, half, send_plan, 0)

    row = lax.broadcasted_iota(jnp.int32, (16, 2 * side), 0)
    lane = lax.broadcasted_iota(jnp.int32, (16, 2 * side), 1)
    ones = jnp.where((row < 8) == (lane < side), 1.0, 0.0).astype(BF16)
    join = jnp.concatenate
    for k in range(chunks):
        copy(k).wait()
        slots = list(range(CHUNKS[k], CHUNKS[k + 1]))
        got = []
        for i in range(0, len(slots), 4):
            t = [tiles_ref[slot] for slot in slots[i:i + 4]]
            sums = tile_product(ones, join([join([t[0], t[1]], 1), join([t[2], t[3]], 1)], 0))
            got += [sums[:8, :side], sums[8:, :side], sums[:8, side:], sums[8:, side:]]
        for t, part in zip(slots, got):
            target = index_ref[0, t]
            if t >= ghosts:
                target = jnp.where(t < count, target, blocks)
            acc_ref[target] += part

    small[2].wait()

    def scale_step(base, _):
        for u in range(8):
            b = base * 8 + u
            factor = lax.rsqrt(1.0 + acc_ref[b])
            scale_ref[b] = factor
            at = pl.ds(pl.multiple_of(b * side, side), side)
            scaled_ref[b] = (join([factor, factor], 0) * start_ref[:, at]).astype(BF16)
        return 0

    lax.fori_loop(0, blocks // 8, scale_step, 0)
    pack(plan_ref, scaled_ref, send_a_ref, send_b_ref)


def split(value):
    high = value.astype(BF16)
    return high, (value - high.astype(F32)).astype(BF16)


def gram_place(level):
    width = 16 * (level + 1)
    first = {4: 0, 2: 80, 3: 128, 1: 192, 0: 224}[level]
    return slice(first, first + width)


def gram_rows(parts, gram_ref, level, prepare):
    rows = parts[0].shape[1]
    chunk = 1024
    width = 16 * (level + 1)
    acc = jnp.zeros((2 * width, 32), F32)
    for k in range(rows // chunk):
        at = slice(k * chunk, (k + 1) * chunk)
        last = prepare(at)
        right = jnp.concatenate([p[:16, at] for p in parts[:-1]] + [last[:16]]
                                + [p[16:, at] for p in parts[:-1]] + [last[16:]], 0)
        acc += lax.dot_general(right, last, (((1,), (1,)), ((), ())), preferred_element_type=F32)
    acc = jnp.concatenate([acc, jnp.zeros((2 * width, 96), F32)], 1)
    if 2 * width % 128:
        acc = jnp.concatenate([acc, jnp.zeros(((-2 * width) % 128, 128), F32)], 0)
    acc = acc.T
    both = acc[:16] + acc[16:32]
    gram_ref[:, gram_place(level)] = both[:, :width] + both[:, width:2 * width]


def own_kernel(level, *refs):
    plan_ref, tiles_ref, scaled_ref, got_ref, vec_ref = refs[:5]
    older = refs[5:5 + level]
    at = 5 + level
    gram_in = None
    if level:
        gram_in = refs[at]
        at += 1
    acc_ref, part_ref, gram_ref = refs[at:at + 3]
    half = got_ref.shape[0]
    acc_ref[...] = jnp.zeros_like(acc_ref)
    ghosts = 2 * half

    spread_tiles(ghosts, 32, acc_ref, lambda t: scaled_ref[plan_ref[OCOL * LIST + t]],
                 lambda t: tiles_ref[ghosts + t], lambda t: plan_ref[OROW * LIST + t])
    spread_tiles(half, 32, acc_ref, lambda g: got_ref[g],
                 lambda g: tiles_ref[plan_ref[SLOT * LIST + g]], lambda g: plan_ref[GROW * LIST + g])
    gram_ref[...] = gram_in[...] if level else jnp.zeros_like(gram_ref)

    def prepare(where):
        stacked = jnp.concatenate(split(vec_ref[:, where]), 0)
        part_ref[:, where] = stacked
        return stacked

    gram_rows(tuple(older) + (part_ref,), gram_ref, level, prepare)


def far_kernel(level, last, *refs):
    plan_ref, tiles_ref, got_ref, _, scale_ref = refs[:5]
    at = 5
    prev_ref = None
    if level > 1:
        prev_ref = refs[at]
        at += 1
    if last:
        older = refs[at:at + level]
        gram_in = refs[at + level]
        at += level + 1
        part_ref, gram_ref, acc_ref = refs[at:at + 3]
    else:
        vec_ref, scaled_ref, send_a_ref, send_b_ref, acc_ref = refs[at:at + 5]
    half = got_ref.shape[0]
    side = tiles_ref.shape[1]
    blocks = scale_ref.shape[0]
    spread_tiles(half, 32, acc_ref, lambda g: got_ref[g],
                 lambda g: tiles_ref[plan_ref[SLOT * LIST + half + g]], lambda g: plan_ref[GROW * LIST + half + g])

    def close(b, where):
        factor = jnp.concatenate([scale_ref[b], scale_ref[b]], 0)
        value = factor * acc_ref[b]
        if level > 1:
            value = 2.0 * value - prev_ref[:, where]
        return factor, value

    if last:
        def prepare(where):
            values = []
            for first in range(where.start, where.stop, side):
                values.append(close(first // side, slice(first, first + side))[1])
            stacked = jnp.concatenate(split(jnp.concatenate(values, 1)), 0)
            part_ref[:, where] = stacked
            return stacked

        gram_ref[...] = gram_in[...]
        gram_rows(tuple(older) + (part_ref,), gram_ref, level, prepare)
        return

    def close_step(base, _):
        for u in range(8):
            b = base * 8 + u
            where = pl.ds(pl.multiple_of(b * side, side), side)
            factor, value = close(b, where)
            vec_ref[:, where] = value
            scaled_ref[b] = (factor * value).astype(BF16)
        return 0

    lax.fori_loop(0, blocks // 8, close_step, 0)
    pack(plan_ref, scaled_ref, send_a_ref, send_b_ref)


def inverse_factor(gram):
    groups = gram.shape[0] // 8
    full = (8, 128)
    row8 = lax.broadcasted_iota(jnp.int32, full, 0)
    lane = lax.broadcasted_iota(jnp.int32, full, 1)
    left = [gram[8 * g:8 * g + 8] for g in range(groups)]
    right = [jnp.where(lane == row8 + 8 * g, 1.0, 0.0) for g in range(groups)]

    def across(value, at):
        return jnp.broadcast_to(value[:, at:at + 1], full)

    def down(value, at):
        return jnp.broadcast_to(value[at:at + 1, :], full)

    def column(entries):
        out = jnp.zeros(full, F32)
        for i, entry in entries:
            out = jnp.where(row8 == i, entry, out)
        return out

    def combine(columns, value):
        return sum(c * down(value, k) for k, c in enumerate(columns))

    done = []
    for p in range(groups):
        a, b = left[p], right[p]
        spread = [across(a, 8 * p + k) for k in range(8)]
        e = [[down(spread[k], i) for k in range(i + 1)] for i in range(8)]
        scale = []
        for k in range(8):
            scale.append(lax.rsqrt(e[k][k]))
            for i in range(k + 1, 8):
                e[i][k] = e[i][k] * scale[k]
            for i in range(k + 1, 8):
                for j in range(k + 1, i + 1):
                    e[i][j] = e[i][j] - e[i][k] * e[j][k]
        m = [[None] * 8 for _ in range(8)]
        for j in range(8):
            m[j][j] = scale[j]
            for i in range(j + 1, 8):
                m[i][j] = -scale[i] * sum(e[i][k] * m[k][j] for k in range(j, i))
        solve = [column([(i, m[i][k]) for i in range(k, 8)]) for k in range(8)]
        ua, ub = combine(solve, a), combine(solve, b)
        done.append(ub)
        if p + 1 < groups:
            back = [column([(k, m[i][k]) for k in range(i + 1)]) for i in range(8)]
            wa, wb = combine(back, ua), combine(back, ub)
            wa, wb = [down(wa, k) for k in range(8)], [down(wb, k) for k in range(8)]
            for g in range(p + 1, groups):
                factors = [across(left[g], 8 * p + k) for k in range(8)]
                left[g] = left[g] - sum(f * w for f, w in zip(factors, wa))
                right[g] = right[g] - sum(f * w for f, w in zip(factors, wb))
    return jnp.concatenate(done, 0)


def final_kernel(row_total, gram_in, *refs):
    parts = refs[:STEPS + 1]
    basis_ref, gram_ref, mix_ref, stage_ref, sems = refs[STEPS + 1:]
    width = gram_ref.shape[0]

    if True:
        groups = [gram_in[:, gram_place(k)] * (1.0 / row_total) for k in range(STEPS + 1)]
        lower = jnp.concatenate(
            [jnp.concatenate([g, jnp.zeros((16, 128 - g.shape[1]), F32)], 1) for g in groups], 0)
        row = lax.broadcasted_iota(jnp.int32, lower.shape, 0)
        lane = lax.broadcasted_iota(jnp.int32, lower.shape, 1)
        lower = jnp.where(row >= lane, lower, 0.0)
        strict = jnp.where(row > lane, lower, 0.0)
        square = jnp.concatenate([strict, jnp.zeros((128 - width, 128), F32)], 0)
        full = lower + square.T[:width]
        gram_ref[...] = full[:, :width]
        inverse = inverse_factor(full)
        high, low = split(inverse[:, :width])
        mix_ref[...] = jnp.concatenate([high, low, high], 1)

    pieces = stage_ref.shape[0]
    chunk = stage_ref.shape[2]

    def out(k):
        return pltpu.make_async_copy(stage_ref.at[k], basis_ref.at[:, pl.ds(k * chunk, chunk)], sems.at[k])

    mix = mix_ref[...]
    for k in range(pieces):
        at = slice(k * chunk, (k + 1) * chunk)
        tops = [p[:16, at] for p in parts]
        lows = [p[16:, at] for p in parts]
        stack = jnp.concatenate(tops + tops + lows, 0)
        stage_ref[k] = jnp.dot(mix, stack, preferred_element_type=F32)
        out(k).start()
    for k in range(pieces):
        out(k).wait()


def params(mib, **kw):
    return pltpu.CompilerParams(vmem_limit_bytes=mib * 2**20, **kw)


def body(start_vectors, tile_index, tile_values, tile_count, ghost_send):
    rows, width = start_vectors.shape
    total, side, _ = tile_values.shape
    blocks = rows // side
    half = ghost_send.shape[2]
    n = lax.axis_size(AXIS)
    basis = width * (STEPS + 1)
    shape = jax.ShapeDtypeStruct

    scaled_t = shape((blocks, width, side), BF16)
    send_t = shape((half, width, side), BF16)
    vec_t = shape((width, rows), F32)
    part_t = shape((2 * width, rows), BF16)
    acc_t = shape((blocks + 1, width, side), F32)
    gram_t = shape((16, 256), F32)

    near = [(i, i ^ 1) for i in range(n)]
    far = [(i, (i + 1) % n if i % 2 else (i - 1) % n) for i in range(n)]

    start = start_vectors.T
    tiles, plan, scale, scaled, send_a, send_b = pl.pallas_call(
        setup_kernel,
        out_shape=(shape((total, side, side), BF16), SMEM((5 * LIST,), jnp.int32),
                   shape((blocks, 8, side), F32), scaled_t, send_t, send_t),
        in_specs=[spec(pltpu.HBM)] * 4 + [spec(SMEM)],
        out_specs=(spec(VMEM), spec(SMEM), spec(VMEM), spec(VMEM), spec(VMEM), spec(VMEM)),
        scratch_shapes=[VMEM((blocks + 1, 8, side), F32), SMEM((2, total), jnp.int32),
                        SMEM((2, half), jnp.int32), VMEM((width, rows), F32), pltpu.SemaphoreType.DMA((len(CHUNKS) + 2,))],
        compiler_params=params(41),
        name="setup",
    )(*[pltpu.with_memory_space_constraint(v, pltpu.HBM)
        for v in (tile_index.T, ghost_send[0], tile_values, start)], tile_count)

    vectors = [start]
    parts = []
    gram = None
    for level in range(1, STEPS + 1):
        last = level == STEPS
        got_b = lax.ppermute(send_b, AXIS, far)
        got_a = lax.ppermute(send_a, AXIS, near)
        args = [plan, tiles, scaled, got_a, vectors[-1]] + parts + ([gram] if gram is not None else [])
        acc, part, gram = pl.pallas_call(
            functools.partial(own_kernel, level - 1),
            out_shape=(acc_t, part_t, gram_t),
            in_specs=[spec(SMEM)] + [spec(VMEM)] * (len(args) - 1),
            out_specs=(spec(VMEM),) * 3,
            compiler_params=params(20),
            cost_estimate=pl.CostEstimate(flops=10**9, bytes_accessed=10**7, transcendentals=0),
            name="own",
        )(*args)
        parts.append(part)
        args = [plan, tiles, got_b, acc, scale]
        if level > 1:
            args.append(vectors[-2])
        if last:
            args += parts + [gram]
            outs = (part_t, gram_t, acc_t)
        else:
            outs = (vec_t, scaled_t, send_t, send_t, acc_t)
        got = pl.pallas_call(
            functools.partial(far_kernel, level, last),
            out_shape=outs,
            in_specs=[spec(SMEM)] + [spec(VMEM)] * (len(args) - 1),
            out_specs=(spec(VMEM),) * len(outs),
            input_output_aliases={3: len(outs) - 1},
            compiler_params=params(20),
            name="far",
        )(*args)
        if last:
            part, gram, _ = got
            parts.append(part)
        else:
            vec, scaled, send_a, send_b, _ = got
            vectors.append(vec)

    def phase(value, shift, count):
        mask = (count - 1) << shift
        moved = value
        for d in range(1, count):
            perm = [(i, (i & ~mask) | ((((i >> shift) + d) & (count - 1)) << shift)) for i in range(n)]
            moved = moved + lax.ppermute(value, AXIS, perm)
        return moved

    for shift, count in ((0, 2), (1, 4), (3, 4), (5, 4)):
        gram = phase(gram, shift, count)

    chunk = 1024
    basis_out, gram_matrix = pl.pallas_call(
        functools.partial(final_kernel, rows * n),
        out_shape=(shape((basis, rows), F32), shape((basis, basis), F32)),
        in_specs=[spec(VMEM)] * (STEPS + 2),
        out_specs=(spec(pltpu.HBM), spec(VMEM)),
        scratch_shapes=[VMEM((basis, 3 * basis), BF16), VMEM((rows // chunk, basis, chunk), F32),
                        pltpu.SemaphoreType.DMA((rows // chunk,))],
        compiler_params=params(20),
        name="final",
    )(gram, *parts)
    return basis_out.T, gram_matrix


def solution(mesh):
    placed = (
        P("parts", None),
        P("parts", None),
        P("parts", None, None),
        P("parts"),
        P("parts", None, None),
    )
    return jax.shard_map(
        body, mesh=mesh, in_specs=placed, out_specs=(P("parts", None), P()), check_vma=False
    )
```

```python
import functools

import jax
import jax.numpy as jnp
from jax import lax
from jax.experimental import pallas as pl
from jax.experimental.pallas import tpu as pltpu
from jax.sharding import PartitionSpec as P

STEPS = 4
AXIS = "parts"
VMEM = pltpu.VMEM
SMEM = pltpu.SMEM
F32 = jnp.float32
BF16 = jnp.bfloat16

SLOT, GROW, OCOL, OROW, SEND = range(5)
LIST = 128
CHUNKS = (0, 128, 256)


def spec(space):
    return pl.BlockSpec(memory_space=space)


def tile_product(block, tile):
    return lax.dot_general(block, tile, (((1,), (1,)), ((), ())), preferred_element_type=F32)


def quad_products(blocks, tiles):
    zero = jnp.zeros_like(blocks[0])
    join = jnp.concatenate
    out = []
    for i in range(0, len(blocks), 4):
        x, t = blocks[i:i + 4], tiles[i:i + 4]
        left = join([join([x[0], zero], 1), join([zero, x[1]], 1), join([x[2], zero], 1), join([zero, x[3]], 1)], 0)
        right = join([join([t[0], t[1]], 1), join([t[2], t[3]], 1)], 0)
        got = tile_product(left, right)
        out += [got[:16, :128], got[16:32, :128], got[32:48, 128:], got[48:, 128:]]
    return out


def spread_tiles(count, unroll, acc_ref, block_at, tile_at, row_at):
    def step(base, _):
        at = [base * unroll + u for u in range(unroll)]
        got = quad_products([block_at(t) for t in at], [tile_at(t) for t in at])
        for t, product in zip(at, got):
            acc_ref[row_at(t)] += product
        return 0

    lax.fori_loop(0, count // unroll, step, 0)


def pack(plan_ref, scaled_ref, send_a_ref, send_b_ref):
    half = send_a_ref.shape[0]

    def step(base, _):
        for u in range(8):
            g = base * 8 + u
            send_b_ref[g] = scaled_ref[plan_ref[SEND * LIST + half + g]]
        for u in range(8):
            g = base * 8 + u
            send_a_ref[g] = scaled_ref[plan_ref[SEND * LIST + g]]
        return 0

    lax.fori_loop(0, half // 8, step, 0)


def setup_kernel(index_in, ghost_in, values_ref, start_in, count_ref,
                 tiles_ref, plan_ref, scale_ref, scaled_ref, send_a_ref, send_b_ref,
                 acc_ref, index_ref, ghost_ref, start_ref, sems):
    total, side = values_ref.shape[0], values_ref.shape[1]
    blocks = scaled_ref.shape[0]
    half = send_a_ref.shape[0]
    ghosts = 2 * half
    chunks = len(CHUNKS) - 1

    def copy(k):
        at = pl.ds(CHUNKS[k], CHUNKS[k + 1] - CHUNKS[k])
        return pltpu.make_async_copy(values_ref.at[at], tiles_ref.at[at], sems.at[k])

    small = [pltpu.make_async_copy(a, b, sems.at[chunks + i]) for i, (a, b) in enumerate(
        ((index_in, index_ref), (ghost_in, ghost_ref), (start_in, start_ref)))]
    for c in small[:2]:
        c.start()
    for k in range(chunks):
        copy(k).start()
    small[2].start()
    for c in small[:2]:
        c.wait()

    odd = lax.rem(lax.axis_index(AXIS), 2)
    flip = (1 - odd) * half
    count = count_ref[0]
    acc_ref[...] = jnp.zeros_like(acc_ref)

    def ghost_plan(base, _):
        for u in range(4):
            t = base * 4 + u
            place = jnp.bitwise_xor(index_ref[1, t] - blocks, flip)
            plan_ref[SLOT * LIST + place] = t
            plan_ref[GROW * LIST + place] = index_ref[0, t]
            plan_ref[OCOL * LIST + t] = index_ref[1, ghosts + t]
            plan_ref[OROW * LIST + t] = jnp.where(ghosts + t < count, index_ref[0, ghosts + t], blocks)
        return 0

    lax.fori_loop(0, ghosts // 4, ghost_plan, 0)

    def send_plan(g, _):
        plan_ref[SEND * LIST + g] = ghost_ref[odd, g]
        plan_ref[SEND * LIST + half + g] = ghost_ref[1 - odd, g]
        return 0

    lax.fori_loop(0, half, send_plan, 0)

    row = lax.broadcasted_iota(jnp.int32, (16, 2 * side), 0)
    lane = lax.broadcasted_iota(jnp.int32, (16, 2 * side), 1)
    ones = jnp.where((row < 8) == (lane < side), 1.0, 0.0).astype(BF16)
    join = jnp.concatenate
    for k in range(chunks):
        copy(k).wait()
        slots = list(range(CHUNKS[k], CHUNKS[k + 1]))
        got = []
        for i in range(0, len(slots), 4):
            t = [tiles_ref[slot] for slot in slots[i:i + 4]]
            sums = tile_product(ones, join([join([t[0], t[1]], 1), join([t[2], t[3]], 1)], 0))
            got += [sums[:8, :side], sums[8:, :side], sums[:8, side:], sums[8:, side:]]
        for t, part in zip(slots, got):
            target = index_ref[0, t]
            if t >= ghosts:
                target = jnp.where(t < count, target, blocks)
            acc_ref[target] += part

    small[2].wait()

    def scale_step(base, _):
        for u in range(8):
            b = base * 8 + u
            factor = lax.rsqrt(1.0 + acc_ref[b])
            scale_ref[b] = factor
            at = pl.ds(pl.multiple_of(b * side, side), side)
            scaled_ref[b] = (join([factor, factor], 0) * start_ref[:, at]).astype(BF16)
        return 0

    lax.fori_loop(0, blocks // 8, scale_step, 0)
    pack(plan_ref, scaled_ref, send_a_ref, send_b_ref)


def split(value):
    high = value.astype(BF16)
    return high, (value - high.astype(F32)).astype(BF16)


def gram_place(level):
    width = 16 * (level + 1)
    first = {4: 0, 2: 80, 3: 128, 1: 192, 0: 224}[level]
    return slice(first, first + width)


def gram_rows(parts, gram_ref, level, prepare):
    rows = parts[0].shape[1]
    chunk = 1024
    width = 16 * (level + 1)
    acc = jnp.zeros((2 * width, 32), F32)
    for k in range(rows // chunk):
        at = slice(k * chunk, (k + 1) * chunk)
        last = prepare(at)
        right = jnp.concatenate([p[:16, at] for p in parts[:-1]] + [last[:16]]
                                + [p[16:, at] for p in parts[:-1]] + [last[16:]], 0)
        acc += lax.dot_general(right, last, (((1,), (1,)), ((), ())), preferred_element_type=F32)
    acc = jnp.concatenate([acc, jnp.zeros((2 * width, 96), F32)], 1)
    if 2 * width % 128:
        acc = jnp.concatenate([acc, jnp.zeros(((-2 * width) % 128, 128), F32)], 0)
    acc = acc.T
    both = acc[:16] + acc[16:32]
    gram_ref[:, gram_place(level)] = both[:, :width] + both[:, width:2 * width]


def own_kernel(level, *refs):
    plan_ref, tiles_ref, scaled_ref, got_ref, vec_ref = refs[:5]
    older = refs[5:5 + level]
    at = 5 + level
    gram_in = None
    if level:
        gram_in = refs[at]
        at += 1
    acc_ref, part_ref, gram_ref = refs[at:at + 3]
    half = got_ref.shape[0]
    acc_ref[...] = jnp.zeros_like(acc_ref)
    ghosts = 2 * half

    spread_tiles(ghosts, 32, acc_ref, lambda t: scaled_ref[plan_ref[OCOL * LIST + t]],
                 lambda t: tiles_ref[ghosts + t], lambda t: plan_ref[OROW * LIST + t])
    spread_tiles(half, 32, acc_ref, lambda g: got_ref[g],
                 lambda g: tiles_ref[plan_ref[SLOT * LIST + g]], lambda g: plan_ref[GROW * LIST + g])
    gram_ref[...] = gram_in[...] if level else jnp.zeros_like(gram_ref)

    def prepare(where):
        stacked = jnp.concatenate(split(vec_ref[:, where]), 0)
        part_ref[:, where] = stacked
        return stacked

    gram_rows(tuple(older) + (part_ref,), gram_ref, level, prepare)


def far_kernel(level, last, *refs):
    plan_ref, tiles_ref, got_ref, _, scale_ref = refs[:5]
    at = 5
    prev_ref = None
    if level > 1:
        prev_ref = refs[at]
        at += 1
    if last:
        older = refs[at:at + level]
        gram_in = refs[at + level]
        at += level + 1
        part_ref, gram_ref, acc_ref = refs[at:at + 3]
    else:
        vec_ref, scaled_ref, send_a_ref, send_b_ref, acc_ref = refs[at:at + 5]
    half = got_ref.shape[0]
    side = tiles_ref.shape[1]
    blocks = scale_ref.shape[0]
    spread_tiles(half, 32, acc_ref, lambda g: got_ref[g],
                 lambda g: tiles_ref[plan_ref[SLOT * LIST + half + g]], lambda g: plan_ref[GROW * LIST + half + g])

    def close(b, where):
        factor = jnp.concatenate([scale_ref[b], scale_ref[b]], 0)
        value = factor * acc_ref[b]
        if level > 1:
            value = 2.0 * value - prev_ref[:, where]
        return factor, value

    if last:
        def prepare(where):
            values = []
            for first in range(where.start, where.stop, side):
                values.append(close(first // side, slice(first, first + side))[1])
            stacked = jnp.concatenate(split(jnp.concatenate(values, 1)), 0)
            part_ref[:, where] = stacked
            return stacked

        gram_ref[...] = gram_in[...]
        gram_rows(tuple(older) + (part_ref,), gram_ref, level, prepare)
        return

    def close_step(base, _):
        for u in range(8):
            b = base * 8 + u
            where = pl.ds(pl.multiple_of(b * side, side), side)
            factor, value = close(b, where)
            vec_ref[:, where] = value
            scaled_ref[b] = (factor * value).astype(BF16)
        return 0

    lax.fori_loop(0, blocks // 8, close_step, 0)
    pack(plan_ref, scaled_ref, send_a_ref, send_b_ref)


def inverse_factor(gram):
    groups = gram.shape[0] // 8
    full = (8, 128)
    row8 = lax.broadcasted_iota(jnp.int32, full, 0)
    lane = lax.broadcasted_iota(jnp.int32, full, 1)
    left = [gram[8 * g:8 * g + 8] for g in range(groups)]
    right = [jnp.where(lane == row8 + 8 * g, 1.0, 0.0) for g in range(groups)]

    def across(value, at):
        return jnp.broadcast_to(value[:, at:at + 1], full)

    def down(value, at):
        return jnp.broadcast_to(value[at:at + 1, :], full)

    def column(entries):
        out = jnp.zeros(full, F32)
        for i, entry in entries:
            out = jnp.where(row8 == i, entry, out)
        return out

    def combine(columns, value):
        return sum(c * down(value, k) for k, c in enumerate(columns))

    done = []
    for p in range(groups):
        a, b = left[p], right[p]
        spread = [across(a, 8 * p + k) for k in range(8)]
        e = [[down(spread[k], i) for k in range(i + 1)] for i in range(8)]
        scale = []
        for k in range(8):
            scale.append(lax.rsqrt(e[k][k]))
            for i in range(k + 1, 8):
                e[i][k] = e[i][k] * scale[k]
            for i in range(k + 1, 8):
                for j in range(k + 1, i + 1):
                    e[i][j] = e[i][j] - e[i][k] * e[j][k]
        m = [[None] * 8 for _ in range(8)]
        for j in range(8):
            m[j][j] = scale[j]
            for i in range(j + 1, 8):
                m[i][j] = -scale[i] * sum(e[i][k] * m[k][j] for k in range(j, i))
        solve = [column([(i, m[i][k]) for i in range(k, 8)]) for k in range(8)]
        ua, ub = combine(solve, a), combine(solve, b)
        done.append(ub)
        if p + 1 < groups:
            back = [column([(k, m[i][k]) for k in range(i + 1)]) for i in range(8)]
            wa, wb = combine(back, ua), combine(back, ub)
            wa, wb = [down(wa, k) for k in range(8)], [down(wb, k) for k in range(8)]
            for g in range(p + 1, groups):
                factors = [across(left[g], 8 * p + k) for k in range(8)]
                left[g] = left[g] - sum(f * w for f, w in zip(factors, wa))
                right[g] = right[g] - sum(f * w for f, w in zip(factors, wb))
    return jnp.concatenate(done, 0)


def final_kernel(row_total, gram_in, *refs):
    parts = refs[:STEPS + 1]
    basis_ref, gram_ref, mix_ref, stage_ref, sems = refs[STEPS + 1:]
    width = gram_ref.shape[0]

    if True:
        groups = [gram_in[:, gram_place(k)] * (1.0 / row_total) for k in range(STEPS + 1)]
        lower = jnp.concatenate(
            [jnp.concatenate([g, jnp.zeros((16, 128 - g.shape[1]), F32)], 1) for g in groups], 0)
        row = lax.broadcasted_iota(jnp.int32, lower.shape, 0)
        lane = lax.broadcasted_iota(jnp.int32, lower.shape, 1)
        lower = jnp.where(row >= lane, lower, 0.0)
        strict = jnp.where(row > lane, lower, 0.0)
        square = jnp.concatenate([strict, jnp.zeros((128 - width, 128), F32)], 0)
        full = lower + square.T[:width]
        gram_ref[...] = full[:, :width]
        inverse = inverse_factor(full)
        high, low = split(inverse[:, :width])
        mix_ref[...] = jnp.concatenate([high, low, high], 1)

    pieces = stage_ref.shape[0]
    chunk = stage_ref.shape[2]

    def out(k):
        return pltpu.make_async_copy(stage_ref.at[k], basis_ref.at[:, pl.ds(k * chunk, chunk)], sems.at[k])

    mix = mix_ref[...]
    for k in range(pieces):
        at = slice(k * chunk, (k + 1) * chunk)
        tops = [p[:16, at] for p in parts]
        lows = [p[16:, at] for p in parts]
        stack = jnp.concatenate(tops + tops + lows, 0)
        stage_ref[k] = jnp.dot(mix, stack, preferred_element_type=F32)
        out(k).start()
    for k in range(pieces):
        out(k).wait()


def params(mib, **kw):
    return pltpu.CompilerParams(vmem_limit_bytes=mib * 2**20, **kw)


def body(start_vectors, tile_index, tile_values, tile_count, ghost_send):
    rows, width = start_vectors.shape
    total, side, _ = tile_values.shape
    blocks = rows // side
    half = ghost_send.shape[2]
    n = lax.axis_size(AXIS)
    basis = width * (STEPS + 1)
    shape = jax.ShapeDtypeStruct

    scaled_t = shape((blocks, width, side), BF16)
    send_t = shape((half, width, side), BF16)
    vec_t = shape((width, rows), F32)
    part_t = shape((2 * width, rows), BF16)
    acc_t = shape((blocks + 1, width, side), F32)
    gram_t = shape((16, 256), F32)

    near = [(i, i ^ 1) for i in range(n)]
    far = [(i, (i + 1) % n if i % 2 else (i - 1) % n) for i in range(n)]

    start = start_vectors.T
    tiles, plan, scale, scaled, send_a, send_b = pl.pallas_call(
        setup_kernel,
        out_shape=(shape((total, side, side), BF16), SMEM((5 * LIST,), jnp.int32),
                   shape((blocks, 8, side), F32), scaled_t, send_t, send_t),
        in_specs=[spec(pltpu.HBM)] * 4 + [spec(SMEM)],
        out_specs=(spec(VMEM), spec(SMEM), spec(VMEM), spec(VMEM), spec(VMEM), spec(VMEM)),
        scratch_shapes=[VMEM((blocks + 1, 8, side), F32), SMEM((2, total), jnp.int32),
                        SMEM((2, half), jnp.int32), VMEM((width, rows), F32), pltpu.SemaphoreType.DMA((len(CHUNKS) + 2,))],
        compiler_params=params(41),
        name="setup",
    )(*[pltpu.with_memory_space_constraint(v, pltpu.HBM)
        for v in (tile_index.T, ghost_send[0], tile_values, start)], tile_count)

    vectors = [start]
    parts = []
    gram = None
    for level in range(1, STEPS + 1):
        last = level == STEPS
        got_b = lax.ppermute(send_b, AXIS, far)
        got_a = lax.ppermute(send_a, AXIS, near)
        args = [plan, tiles, scaled, got_a, vectors[-1]] + parts + ([gram] if gram is not None else [])
        acc, part, gram = pl.pallas_call(
            functools.partial(own_kernel, level - 1),
            out_shape=(acc_t, part_t, gram_t),
            in_specs=[spec(SMEM)] + [spec(VMEM)] * (len(args) - 1),
            out_specs=(spec(VMEM),) * 3,
            compiler_params=params(20),
            cost_estimate=pl.CostEstimate(flops=10**9, bytes_accessed=10**7, transcendentals=0),
            name="own",
        )(*args)
        parts.append(part)
        args = [plan, tiles, got_b, acc, scale]
        if level > 1:
            args.append(vectors[-2])
        if last:
            args += parts + [gram]
            outs = (part_t, gram_t, acc_t)
        else:
            outs = (vec_t, scaled_t, send_t, send_t, acc_t)
        got = pl.pallas_call(
            functools.partial(far_kernel, level, last),
            out_shape=outs,
            in_specs=[spec(SMEM)] + [spec(VMEM)] * (len(args) - 1),
            out_specs=(spec(VMEM),) * len(outs),
            input_output_aliases={3: len(outs) - 1},
            compiler_params=params(20),
            name="far",
        )(*args)
        if last:
            part, gram, _ = got
            parts.append(part)
        else:
            vec, scaled, send_a, send_b, _ = got
            vectors.append(vec)

    def phase(value, shift, count, upward):
        mask = (count - 1) << shift
        moved = value
        for d in range(count - 1, 0, -1):
            perm = []
            for i in range(n):
                step = d if upward(i) else count - d
                perm.append((i, (i & ~mask) | ((((i >> shift) + step) & (count - 1)) << shift)))
            moved = moved + lax.ppermute(value, AXIS, perm)
        return moved

    def high_z(i):
        return i >= n // 2

    def high_y(i):
        return (i >> 4) & 1 == 1

    for shift, count, upward in ((0, 2, high_z), (1, 4, high_z), (3, 4, high_z), (5, 4, high_y)):
        gram = phase(gram, shift, count, upward)

    chunk = 1024
    basis_out, gram_matrix = pl.pallas_call(
        functools.partial(final_kernel, rows * n),
        out_shape=(shape((basis, rows), F32), shape((basis, basis), F32)),
        in_specs=[spec(VMEM)] * (STEPS + 2),
        out_specs=(spec(pltpu.HBM), spec(VMEM)),
        scratch_shapes=[VMEM((basis, 3 * basis), BF16), VMEM((rows // chunk, basis, chunk), F32),
                        pltpu.SemaphoreType.DMA((rows // chunk,))],
        compiler_params=params(20),
        name="final",
    )(gram, *parts)
    return basis_out.T, gram_matrix


def solution(mesh):
    placed = (
        P("parts", None),
        P("parts", None),
        P("parts", None, None),
        P("parts"),
        P("parts", None, None),
    )
    return jax.shard_map(
        body, mesh=mesh, in_specs=placed, out_specs=(P("parts", None), P()), check_vma=False
    )
```

```python
import functools

import jax
import jax.numpy as jnp
from jax import lax
from jax.experimental import pallas as pl
from jax.experimental.pallas import tpu as pltpu
from jax.sharding import PartitionSpec as P

STEPS = 4
AXIS = "parts"
VMEM = pltpu.VMEM
SMEM = pltpu.SMEM
F32 = jnp.float32
BF16 = jnp.bfloat16

SLOT, GROW, OCOL, OROW, SEND = range(5)
LIST = 128
CHUNKS = (0, 128, 256)


def spec(space):
    return pl.BlockSpec(memory_space=space)


def tile_product(block, tile):
    return lax.dot_general(block, tile, (((1,), (1,)), ((), ())), preferred_element_type=F32)


def quad_products(blocks, tiles):
    zero = jnp.zeros_like(blocks[0])
    join = jnp.concatenate
    out = []
    for i in range(0, len(blocks), 4):
        x, t = blocks[i:i + 4], tiles[i:i + 4]
        left = join([join([x[0], zero], 1), join([zero, x[1]], 1), join([x[2], zero], 1), join([zero, x[3]], 1)], 0)
        right = join([join([t[0], t[1]], 1), join([t[2], t[3]], 1)], 0)
        got = tile_product(left, right)
        out += [got[:16, :128], got[16:32, :128], got[32:48, 128:], got[48:, 128:]]
    return out


def spread_tiles(count, unroll, acc_ref, block_at, tile_at, row_at):
    def step(base, _):
        at = [base * unroll + u for u in range(unroll)]
        got = quad_products([block_at(t) for t in at], [tile_at(t) for t in at])
        for t, product in zip(at, got):
            acc_ref[row_at(t)] += product
        return 0

    lax.fori_loop(0, count // unroll, step, 0)


def pack(plan_ref, scaled_ref, send_a_ref, send_b_ref):
    half = send_a_ref.shape[0]

    def step(base, _):
        for u in range(16):
            g = base * 16 + u
            send_b_ref[g] = scaled_ref[plan_ref[SEND * LIST + half + g]]
        for u in range(16):
            g = base * 16 + u
            send_a_ref[g] = scaled_ref[plan_ref[SEND * LIST + g]]
        return 0

    lax.fori_loop(0, half // 16, step, 0)


def setup_kernel(index_in, ghost_in, values_ref, start_in, count_ref,
                 tiles_ref, plan_ref, scale_ref, scaled_ref, send_a_ref, send_b_ref,
                 acc_ref, index_ref, ghost_ref, start_ref, sems):
    total, side = values_ref.shape[0], values_ref.shape[1]
    blocks = scaled_ref.shape[0]
    half = send_a_ref.shape[0]
    ghosts = 2 * half
    chunks = len(CHUNKS) - 1

    def copy(k):
        at = pl.ds(CHUNKS[k], CHUNKS[k + 1] - CHUNKS[k])
        return pltpu.make_async_copy(values_ref.at[at], tiles_ref.at[at], sems.at[k])

    small = [pltpu.make_async_copy(a, b, sems.at[chunks + i]) for i, (a, b) in enumerate(
        ((index_in, index_ref), (ghost_in, ghost_ref), (start_in, start_ref)))]
    for c in small[:2]:
        c.start()
    for k in range(chunks):
        copy(k).start()
    small[2].start()
    for c in small[:2]:
        c.wait()

    odd = lax.rem(lax.axis_index(AXIS), 2)
    flip = (1 - odd) * half
    count = count_ref[0]
    acc_ref[...] = jnp.zeros_like(acc_ref)

    def ghost_plan(base, _):
        for u in range(4):
            t = base * 4 + u
            place = jnp.bitwise_xor(index_ref[1, t] - blocks, flip)
            plan_ref[SLOT * LIST + place] = t
            plan_ref[GROW * LIST + place] = index_ref[0, t]
            plan_ref[OCOL * LIST + t] = index_ref[1, ghosts + t]
            plan_ref[OROW * LIST + t] = jnp.where(ghosts + t < count, index_ref[0, ghosts + t], blocks)
        return 0

    lax.fori_loop(0, ghosts // 4, ghost_plan, 0)

    def send_plan(g, _):
        plan_ref[SEND * LIST + g] = ghost_ref[odd, g]
        plan_ref[SEND * LIST + half + g] = ghost_ref[1 - odd, g]
        return 0

    lax.fori_loop(0, half, send_plan, 0)

    row = lax.broadcasted_iota(jnp.int32, (16, 2 * side), 0)
    lane = lax.broadcasted_iota(jnp.int32, (16, 2 * side), 1)
    ones = jnp.where((row < 8) == (lane < side), 1.0, 0.0).astype(BF16)
    join = jnp.concatenate
    for k in range(chunks):
        copy(k).wait()
        slots = list(range(CHUNKS[k], CHUNKS[k + 1]))
        got = []
        for i in range(0, len(slots), 4):
            t = [tiles_ref[slot] for slot in slots[i:i + 4]]
            sums = tile_product(ones, join([join([t[0], t[1]], 1), join([t[2], t[3]], 1)], 0))
            got += [sums[:8, :side], sums[8:, :side], sums[:8, side:], sums[8:, side:]]
        for t, part in zip(slots, got):
            target = index_ref[0, t]
            if t >= ghosts:
                target = jnp.where(t < count, target, blocks)
            acc_ref[target] += part

    small[2].wait()

    def scale_step(base, _):
        for u in range(8):
            b = base * 8 + u
            factor = lax.rsqrt(1.0 + acc_ref[b])
            scale_ref[b] = factor
            at = pl.ds(pl.multiple_of(b * side, side), side)
            scaled_ref[b] = (join([factor, factor], 0) * start_ref[:, at]).astype(BF16)
        return 0

    lax.fori_loop(0, blocks // 8, scale_step, 0)
    pack(plan_ref, scaled_ref, send_a_ref, send_b_ref)


def split(value):
    high = value.astype(BF16)
    return high, (value - high.astype(F32)).astype(BF16)


def gram_place(level):
    width = 16 * (level + 1)
    first = {4: 0, 2: 80, 3: 128, 1: 192, 0: 224}[level]
    return slice(first, first + width)


def gram_rows(parts, gram_ref, level, prepare):
    rows = parts[0].shape[1]
    chunk = 1024
    width = 16 * (level + 1)
    acc = jnp.zeros((2 * width, 32), F32)
    for k in range(rows // chunk):
        at = slice(k * chunk, (k + 1) * chunk)
        last = prepare(at)
        right = jnp.concatenate([p[:16, at] for p in parts[:-1]] + [last[:16]]
                                + [p[16:, at] for p in parts[:-1]] + [last[16:]], 0)
        acc += lax.dot_general(right, last, (((1,), (1,)), ((), ())), preferred_element_type=F32)
    acc = jnp.concatenate([acc, jnp.zeros((2 * width, 96), F32)], 1)
    if 2 * width % 128:
        acc = jnp.concatenate([acc, jnp.zeros(((-2 * width) % 128, 128), F32)], 0)
    acc = acc.T
    both = acc[:16] + acc[16:32]
    gram_ref[:, gram_place(level)] = both[:, :width] + both[:, width:2 * width]


def own_kernel(level, *refs):
    plan_ref, tiles_ref, scaled_ref, got_ref, vec_ref = refs[:5]
    older = refs[5:5 + level]
    at = 5 + level
    gram_in = None
    if level:
        gram_in = refs[at]
        at += 1
    acc_ref, part_ref, gram_ref = refs[at:at + 3]
    half = got_ref.shape[0]
    acc_ref[...] = jnp.zeros_like(acc_ref)
    ghosts = 2 * half

    spread_tiles(ghosts, 32, acc_ref, lambda t: scaled_ref[plan_ref[OCOL * LIST + t]],
                 lambda t: tiles_ref[ghosts + t], lambda t: plan_ref[OROW * LIST + t])
    spread_tiles(half, 32, acc_ref, lambda g: got_ref[g],
                 lambda g: tiles_ref[plan_ref[SLOT * LIST + g]], lambda g: plan_ref[GROW * LIST + g])
    gram_ref[...] = gram_in[...] if level else jnp.zeros_like(gram_ref)

    def prepare(where):
        stacked = jnp.concatenate(split(vec_ref[:, where]), 0)
        part_ref[:, where] = stacked
        return stacked

    gram_rows(tuple(older) + (part_ref,), gram_ref, level, prepare)


def far_kernel(level, last, *refs):
    plan_ref, tiles_ref, got_ref, _, scale_ref = refs[:5]
    at = 5
    prev_ref = None
    if level > 1:
        prev_ref = refs[at]
        at += 1
    if last:
        older = refs[at:at + level]
        gram_in = refs[at + level]
        at += level + 1
        part_ref, gram_ref, acc_ref = refs[at:at + 3]
    else:
        vec_ref, scaled_ref, send_a_ref, send_b_ref, acc_ref = refs[at:at + 5]
    half = got_ref.shape[0]
    side = tiles_ref.shape[1]
    blocks = scale_ref.shape[0]
    spread_tiles(half, 32 if last else 64, acc_ref, lambda g: got_ref[g],
                 lambda g: tiles_ref[plan_ref[SLOT * LIST + half + g]], lambda g: plan_ref[GROW * LIST + half + g])

    def close(b, where):
        factor = jnp.concatenate([scale_ref[b], scale_ref[b]], 0)
        value = factor * acc_ref[b]
        if level > 1:
            value = 2.0 * value - prev_ref[:, where]
        return factor, value

    if last:
        def prepare(where):
            values = []
            for first in range(where.start, where.stop, side):
                values.append(close(first // side, slice(first, first + side))[1])
            stacked = jnp.concatenate(split(jnp.concatenate(values, 1)), 0)
            part_ref[:, where] = stacked
            return stacked

        gram_ref[...] = gram_in[...]
        gram_rows(tuple(older) + (part_ref,), gram_ref, level, prepare)
        return

    def close_step(base, _):
        for u in range(16):
            b = base * 16 + u
            where = pl.ds(pl.multiple_of(b * side, side), side)
            factor, value = close(b, where)
            vec_ref[:, where] = value
            scaled_ref[b] = (factor * value).astype(BF16)
        return 0

    lax.fori_loop(0, blocks // 16, close_step, 0)
    pack(plan_ref, scaled_ref, send_a_ref, send_b_ref)


def inverse_factor(gram):
    groups = gram.shape[0] // 8
    full = (8, 128)
    row8 = lax.broadcasted_iota(jnp.int32, full, 0)
    lane = lax.broadcasted_iota(jnp.int32, full, 1)
    left = [gram[8 * g:8 * g + 8] for g in range(groups)]
    right = [jnp.where(lane == row8 + 8 * g, 1.0, 0.0) for g in range(groups)]

    def across(value, at):
        return jnp.broadcast_to(value[:, at:at + 1], full)

    def down(value, at):
        return jnp.broadcast_to(value[at:at + 1, :], full)

    def column(entries):
        out = jnp.zeros(full, F32)
        for i, entry in entries:
            out = jnp.where(row8 == i, entry, out)
        return out

    def combine(columns, value):
        return sum(c * down(value, k) for k, c in enumerate(columns))

    done = []
    for p in range(groups):
        a, b = left[p], right[p]
        spread = [across(a, 8 * p + k) for k in range(8)]
        e = [[down(spread[k], i) for k in range(i + 1)] for i in range(8)]
        scale = []
        for k in range(8):
            scale.append(lax.rsqrt(e[k][k]))
            for i in range(k + 1, 8):
                e[i][k] = e[i][k] * scale[k]
            for i in range(k + 1, 8):
                for j in range(k + 1, i + 1):
                    e[i][j] = e[i][j] - e[i][k] * e[j][k]
        m = [[None] * 8 for _ in range(8)]
        for j in range(8):
            m[j][j] = scale[j]
            for i in range(j + 1, 8):
                m[i][j] = -scale[i] * sum(e[i][k] * m[k][j] for k in range(j, i))
        solve = [column([(i, m[i][k]) for i in range(k, 8)]) for k in range(8)]
        ua, ub = combine(solve, a), combine(solve, b)
        done.append(ub)
        if p + 1 < groups:
            back = [column([(k, m[i][k]) for k in range(i + 1)]) for i in range(8)]
            wa, wb = combine(back, ua), combine(back, ub)
            wa, wb = [down(wa, k) for k in range(8)], [down(wb, k) for k in range(8)]
            for g in range(p + 1, groups):
                factors = [across(left[g], 8 * p + k) for k in range(8)]
                left[g] = left[g] - sum(f * w for f, w in zip(factors, wa))
                right[g] = right[g] - sum(f * w for f, w in zip(factors, wb))
    return jnp.concatenate(done, 0)


def final_kernel(row_total, gram_in, *refs):
    parts = refs[:STEPS + 1]
    basis_ref, gram_ref, mix_ref, stage_ref, sems = refs[STEPS + 1:]
    width = gram_ref.shape[0]

    if True:
        groups = [gram_in[:, gram_place(k)] * (1.0 / row_total) for k in range(STEPS + 1)]
        lower = jnp.concatenate(
            [jnp.concatenate([g, jnp.zeros((16, 128 - g.shape[1]), F32)], 1) for g in groups], 0)
        row = lax.broadcasted_iota(jnp.int32, lower.shape, 0)
        lane = lax.broadcasted_iota(jnp.int32, lower.shape, 1)
        lower = jnp.where(row >= lane, lower, 0.0)
        strict = jnp.where(row > lane, lower, 0.0)
        square = jnp.concatenate([strict, jnp.zeros((128 - width, 128), F32)], 0)
        full = lower + square.T[:width]
        gram_ref[...] = full[:, :width]
        inverse = inverse_factor(full)
        high, low = split(inverse[:, :width])
        mix_ref[...] = jnp.concatenate([high, low, high], 1)

    pieces = stage_ref.shape[0]
    chunk = stage_ref.shape[2]

    def out(k):
        return pltpu.make_async_copy(stage_ref.at[k], basis_ref.at[:, pl.ds(k * chunk, chunk)], sems.at[k])

    mix = mix_ref[...]
    for k in range(pieces):
        at = slice(k * chunk, (k + 1) * chunk)
        tops = [p[:16, at] for p in parts]
        lows = [p[16:, at] for p in parts]
        stack = jnp.concatenate(tops + tops + lows, 0)
        stage_ref[k] = jnp.dot(mix, stack, preferred_element_type=F32)
        out(k).start()
    for k in range(pieces):
        out(k).wait()


def params(mib, **kw):
    return pltpu.CompilerParams(vmem_limit_bytes=mib * 2**20, **kw)


def body(start_vectors, tile_index, tile_values, tile_count, ghost_send):
    rows, width = start_vectors.shape
    total, side, _ = tile_values.shape
    blocks = rows // side
    half = ghost_send.shape[2]
    n = lax.axis_size(AXIS)
    basis = width * (STEPS + 1)
    shape = jax.ShapeDtypeStruct

    scaled_t = shape((blocks, width, side), BF16)
    send_t = shape((half, width, side), BF16)
    vec_t = shape((width, rows), F32)
    part_t = shape((2 * width, rows), BF16)
    acc_t = shape((blocks + 1, width, side), F32)
    gram_t = shape((16, 256), F32)

    near = [(i, i ^ 1) for i in range(n)]
    far = [(i, (i + 1) % n if i % 2 else (i - 1) % n) for i in range(n)]

    start = start_vectors.T
    tiles, plan, scale, scaled, send_a, send_b = pl.pallas_call(
        setup_kernel,
        out_shape=(shape((total, side, side), BF16), SMEM((5 * LIST,), jnp.int32),
                   shape((blocks, 8, side), F32), scaled_t, send_t, send_t),
        in_specs=[spec(pltpu.HBM)] * 4 + [spec(SMEM)],
        out_specs=(spec(VMEM), spec(SMEM), spec(VMEM), spec(VMEM), spec(VMEM), spec(VMEM)),
        scratch_shapes=[VMEM((blocks + 1, 8, side), F32), SMEM((2, total), jnp.int32),
                        SMEM((2, half), jnp.int32), VMEM((width, rows), F32), pltpu.SemaphoreType.DMA((len(CHUNKS) + 2,))],
        compiler_params=params(41),
        name="setup",
    )(*[pltpu.with_memory_space_constraint(v, pltpu.HBM)
        for v in (tile_index.T, ghost_send[0], tile_values, start)], tile_count)

    vectors = [start]
    parts = []
    gram = None
    for level in range(1, STEPS + 1):
        last = level == STEPS
        got_b = lax.ppermute(send_b, AXIS, far)
        got_a = lax.ppermute(send_a, AXIS, near)
        args = [plan, tiles, scaled, got_a, vectors[-1]] + parts + ([gram] if gram is not None else [])
        acc, part, gram = pl.pallas_call(
            functools.partial(own_kernel, level - 1),
            out_shape=(acc_t, part_t, gram_t),
            in_specs=[spec(SMEM)] + [spec(VMEM)] * (len(args) - 1),
            out_specs=(spec(VMEM),) * 3,
            compiler_params=params(20),
            cost_estimate=pl.CostEstimate(flops=10**9, bytes_accessed=10**7, transcendentals=0),
            name="own",
        )(*args)
        parts.append(part)
        args = [plan, tiles, got_b, acc, scale]
        if level > 1:
            args.append(vectors[-2])
        if last:
            args += parts + [gram]
            outs = (part_t, gram_t, acc_t)
        else:
            outs = (vec_t, scaled_t, send_t, send_t, acc_t)
        got = pl.pallas_call(
            functools.partial(far_kernel, level, last),
            out_shape=outs,
            in_specs=[spec(SMEM)] + [spec(VMEM)] * (len(args) - 1),
            out_specs=(spec(VMEM),) * len(outs),
            input_output_aliases={3: len(outs) - 1},
            compiler_params=params(20),
            name="far",
        )(*args)
        if last:
            part, gram, _ = got
            parts.append(part)
        else:
            vec, scaled, send_a, send_b, _ = got
            vectors.append(vec)

    def phase(value, shift, count, upward):
        mask = (count - 1) << shift
        moved = value
        for d in range(count - 1, 0, -1):
            perm = []
            for i in range(n):
                step = d if upward(i) else count - d
                perm.append((i, (i & ~mask) | ((((i >> shift) + step) & (count - 1)) << shift)))
            moved = moved + lax.ppermute(value, AXIS, perm)
        return moved

    def high_z(i):
        return i >= n // 2

    def high_y(i):
        return (i >> 4) & 1 == 1

    for shift, count, upward in ((0, 2, high_z), (1, 4, high_z), (3, 4, high_z), (5, 4, high_y)):
        gram = phase(gram, shift, count, upward)

    chunk = 1024
    basis_out, gram_matrix = pl.pallas_call(
        functools.partial(final_kernel, rows * n),
        out_shape=(shape((basis, rows), F32), shape((basis, basis), F32)),
        in_specs=[spec(VMEM)] * (STEPS + 2),
        out_specs=(spec(pltpu.HBM), spec(VMEM)),
        scratch_shapes=[VMEM((basis, 3 * basis), BF16), VMEM((rows // chunk, basis, chunk), F32),
                        pltpu.SemaphoreType.DMA((rows // chunk,))],
        compiler_params=params(20),
        name="final",
    )(gram, *parts)
    return basis_out.T, gram_matrix


def solution(mesh):
    placed = (
        P("parts", None),
        P("parts", None),
        P("parts", None, None),
        P("parts"),
        P("parts", None, None),
    )
    return jax.shard_map(
        body, mesh=mesh, in_specs=placed, out_specs=(P("parts", None), P()), check_vma=False
    )
```

```python
import functools

import jax
import jax.numpy as jnp
from jax import lax
from jax.experimental import pallas as pl
from jax.experimental.pallas import tpu as pltpu
from jax.sharding import PartitionSpec as P

STEPS = 4
AXIS = "parts"
VMEM = pltpu.VMEM
SMEM = pltpu.SMEM
F32 = jnp.float32
BF16 = jnp.bfloat16

SLOT, GROW, OCOL, OROW, SEND = range(5)
LIST = 128
CHUNKS = (0, 128, 256)


def spec(space):
    return pl.BlockSpec(memory_space=space)


def tile_product(block, tile):
    return lax.dot_general(block, tile, (((1,), (1,)), ((), ())), preferred_element_type=F32)


def quad_products(blocks, tiles):
    zero = jnp.zeros_like(blocks[0])
    join = jnp.concatenate
    out = []
    for i in range(0, len(blocks), 4):
        x, t = blocks[i:i + 4], tiles[i:i + 4]
        left = join([join([x[0], zero], 1), join([zero, x[1]], 1), join([x[2], zero], 1), join([zero, x[3]], 1)], 0)
        right = join([join([t[0], t[1]], 1), join([t[2], t[3]], 1)], 0)
        got = tile_product(left, right)
        out += [got[:16, :128], got[16:32, :128], got[32:48, 128:], got[48:, 128:]]
    return out


def spread_tiles(count, unroll, acc_ref, block_at, tile_at, row_at):
    def step(base, _):
        at = [base * unroll + u for u in range(unroll)]
        got = quad_products([block_at(t) for t in at], [tile_at(t) for t in at])
        for t, product in zip(at, got):
            acc_ref[row_at(t)] += product
        return 0

    lax.fori_loop(0, count // unroll, step, 0)


def pack(plan_ref, scaled_ref, send_a_ref, send_b_ref):
    half = send_a_ref.shape[0]

    def step(base, _):
        for u in range(16):
            g = base * 16 + u
            send_b_ref[g] = scaled_ref[plan_ref[SEND * LIST + half + g]]
        for u in range(16):
            g = base * 16 + u
            send_a_ref[g] = scaled_ref[plan_ref[SEND * LIST + g]]
        return 0

    lax.fori_loop(0, half // 16, step, 0)


def setup_kernel(index_in, ghost_in, values_ref, start_in, count_ref,
                 tiles_ref, plan_ref, scale_ref, scaled_ref, send_a_ref, send_b_ref,
                 acc_ref, index_ref, ghost_ref, start_ref, sems):
    total, side = values_ref.shape[0], values_ref.shape[1]
    blocks = scaled_ref.shape[0]
    half = send_a_ref.shape[0]
    ghosts = 2 * half
    chunks = len(CHUNKS) - 1

    def copy(k):
        at = pl.ds(CHUNKS[k], CHUNKS[k + 1] - CHUNKS[k])
        return pltpu.make_async_copy(values_ref.at[at], tiles_ref.at[at], sems.at[k])

    small = [pltpu.make_async_copy(a, b, sems.at[chunks + i]) for i, (a, b) in enumerate(
        ((index_in, index_ref), (ghost_in, ghost_ref), (start_in, start_ref)))]
    for c in small[:2]:
        c.start()
    for k in range(chunks):
        copy(k).start()
    small[2].start()
    for c in small[:2]:
        c.wait()

    odd = lax.rem(lax.axis_index(AXIS), 2)
    flip = (1 - odd) * half
    count = count_ref[0]
    acc_ref[...] = jnp.zeros_like(acc_ref)

    def ghost_plan(base, _):
        for u in range(4):
            t = base * 4 + u
            place = jnp.bitwise_xor(index_ref[1, t] - blocks, flip)
            plan_ref[SLOT * LIST + place] = t
            plan_ref[GROW * LIST + place] = index_ref[0, t]
            plan_ref[OCOL * LIST + t] = index_ref[1, ghosts + t]
            plan_ref[OROW * LIST + t] = jnp.where(ghosts + t < count, index_ref[0, ghosts + t], blocks)
        return 0

    lax.fori_loop(0, ghosts // 4, ghost_plan, 0)

    def send_plan(g, _):
        plan_ref[SEND * LIST + g] = ghost_ref[odd, g]
        plan_ref[SEND * LIST + half + g] = ghost_ref[1 - odd, g]
        return 0

    lax.fori_loop(0, half, send_plan, 0)

    row = lax.broadcasted_iota(jnp.int32, (16, 2 * side), 0)
    lane = lax.broadcasted_iota(jnp.int32, (16, 2 * side), 1)
    ones = jnp.where((row < 8) == (lane < side), 1.0, 0.0).astype(BF16)
    join = jnp.concatenate
    for k in range(chunks):
        copy(k).wait()
        slots = list(range(CHUNKS[k], CHUNKS[k + 1]))
        got = []
        for i in range(0, len(slots), 4):
            t = [tiles_ref[slot] for slot in slots[i:i + 4]]
            sums = tile_product(ones, join([join([t[0], t[1]], 1), join([t[2], t[3]], 1)], 0))
            got += [sums[:8, :side], sums[8:, :side], sums[:8, side:], sums[8:, side:]]
        for t, part in zip(slots, got):
            target = index_ref[0, t]
            if t >= ghosts:
                target = jnp.where(t < count, target, blocks)
            acc_ref[target] += part

    small[2].wait()

    def scale_step(base, _):
        for u in range(16):
            b = base * 16 + u
            factor = lax.rsqrt(1.0 + acc_ref[b])
            scale_ref[b] = factor
            at = pl.ds(pl.multiple_of(b * side, side), side)
            scaled_ref[b] = (join([factor, factor], 0) * start_ref[:, at]).astype(BF16)
        return 0

    lax.fori_loop(0, blocks // 16, scale_step, 0)
    pack(plan_ref, scaled_ref, send_a_ref, send_b_ref)


def split(value):
    high = value.astype(BF16)
    return high, (value - high.astype(F32)).astype(BF16)


def gram_place(level):
    width = 16 * (level + 1)
    first = {4: 0, 2: 80, 3: 128, 1: 192, 0: 224}[level]
    return slice(first, first + width)


def gram_rows(parts, gram_ref, level, prepare):
    rows = parts[0].shape[1]
    chunk = 1024
    width = 16 * (level + 1)
    acc = jnp.zeros((2 * width, 32), F32)
    for k in range(rows // chunk):
        at = slice(k * chunk, (k + 1) * chunk)
        last = prepare(at)
        right = jnp.concatenate([p[:16, at] for p in parts[:-1]] + [last[:16]]
                                + [p[16:, at] for p in parts[:-1]] + [last[16:]], 0)
        acc += lax.dot_general(right, last, (((1,), (1,)), ((), ())), preferred_element_type=F32)
    acc = jnp.concatenate([acc, jnp.zeros((2 * width, 96), F32)], 1)
    if 2 * width % 128:
        acc = jnp.concatenate([acc, jnp.zeros(((-2 * width) % 128, 128), F32)], 0)
    acc = acc.T
    both = acc[:16] + acc[16:32]
    gram_ref[:, gram_place(level)] = both[:, :width] + both[:, width:2 * width]


def own_kernel(level, *refs):
    plan_ref, tiles_ref, scaled_ref, got_ref, vec_ref = refs[:5]
    older = refs[5:5 + level]
    at = 5 + level
    gram_in = None
    if level:
        gram_in = refs[at]
        at += 1
    acc_ref, part_ref, gram_ref = refs[at:at + 3]
    half = got_ref.shape[0]
    acc_ref[...] = jnp.zeros_like(acc_ref)
    ghosts = 2 * half

    spread_tiles(ghosts, 32, acc_ref, lambda t: scaled_ref[plan_ref[OCOL * LIST + t]],
                 lambda t: tiles_ref[ghosts + t], lambda t: plan_ref[OROW * LIST + t])
    spread_tiles(half, 32, acc_ref, lambda g: got_ref[g],
                 lambda g: tiles_ref[plan_ref[SLOT * LIST + g]], lambda g: plan_ref[GROW * LIST + g])
    gram_ref[...] = gram_in[...] if level else jnp.zeros_like(gram_ref)

    def prepare(where):
        stacked = jnp.concatenate(split(vec_ref[:, where]), 0)
        part_ref[:, where] = stacked
        return stacked

    gram_rows(tuple(older) + (part_ref,), gram_ref, level, prepare)


def far_kernel(level, last, *refs):
    plan_ref, tiles_ref, got_ref, _, scale_ref = refs[:5]
    at = 5
    prev_ref = None
    if level > 1:
        prev_ref = refs[at]
        at += 1
    if last:
        older = refs[at:at + level]
        gram_in = refs[at + level]
        at += level + 1
        part_ref, gram_ref, acc_ref = refs[at:at + 3]
    else:
        vec_ref, scaled_ref, send_a_ref, send_b_ref, acc_ref = refs[at:at + 5]
    half = got_ref.shape[0]
    side = tiles_ref.shape[1]
    blocks = scale_ref.shape[0]
    spread_tiles(half, 32 if last else 64, acc_ref, lambda g: got_ref[g],
                 lambda g: tiles_ref[plan_ref[SLOT * LIST + half + g]], lambda g: plan_ref[GROW * LIST + half + g])

    def close(b, where):
        factor = jnp.concatenate([scale_ref[b], scale_ref[b]], 0)
        value = factor * acc_ref[b]
        if level > 1:
            value = 2.0 * value - prev_ref[:, where]
        return factor, value

    if last:
        def prepare(where):
            values = []
            for first in range(where.start, where.stop, side):
                values.append(close(first // side, slice(first, first + side))[1])
            stacked = jnp.concatenate(split(jnp.concatenate(values, 1)), 0)
            part_ref[:, where] = stacked
            return stacked

        gram_ref[...] = gram_in[...]
        gram_rows(tuple(older) + (part_ref,), gram_ref, level, prepare)
        return

    def close_step(base, _):
        for u in range(16):
            b = base * 16 + u
            where = pl.ds(pl.multiple_of(b * side, side), side)
            factor, value = close(b, where)
            vec_ref[:, where] = value
            scaled_ref[b] = (factor * value).astype(BF16)
        return 0

    lax.fori_loop(0, blocks // 16, close_step, 0)
    pack(plan_ref, scaled_ref, send_a_ref, send_b_ref)


def inverse_factor(gram):
    groups = gram.shape[0] // 8
    full = (8, 128)
    row8 = lax.broadcasted_iota(jnp.int32, full, 0)
    lane = lax.broadcasted_iota(jnp.int32, full, 1)
    left = [gram[8 * g:8 * g + 8] for g in range(groups)]
    right = [jnp.where(lane == row8 + 8 * g, 1.0, 0.0) for g in range(groups)]

    def across(value, at):
        return jnp.broadcast_to(value[:, at:at + 1], full)

    def down(value, at):
        return jnp.broadcast_to(value[at:at + 1, :], full)

    def column(entries):
        out = jnp.zeros(full, F32)
        for i, entry in entries:
            out = jnp.where(row8 == i, entry, out)
        return out

    def combine(columns, value):
        return sum(c * down(value, k) for k, c in enumerate(columns))

    done = []
    for p in range(groups):
        a, b = left[p], right[p]
        spread = [across(a, 8 * p + k) for k in range(8)]
        e = [[down(spread[k], i) for k in range(i + 1)] for i in range(8)]
        scale = []
        for k in range(8):
            scale.append(lax.rsqrt(e[k][k]))
            for i in range(k + 1, 8):
                e[i][k] = e[i][k] * scale[k]
            for i in range(k + 1, 8):
                for j in range(k + 1, i + 1):
                    e[i][j] = e[i][j] - e[i][k] * e[j][k]
        m = [[None] * 8 for _ in range(8)]
        for j in range(8):
            m[j][j] = scale[j]
            for i in range(j + 1, 8):
                m[i][j] = -scale[i] * sum(e[i][k] * m[k][j] for k in range(j, i))
        solve = [column([(i, m[i][k]) for i in range(k, 8)]) for k in range(8)]
        ua, ub = combine(solve, a), combine(solve, b)
        done.append(ub)
        if p + 1 < groups:
            back = [column([(k, m[i][k]) for k in range(i + 1)]) for i in range(8)]
            wa, wb = combine(back, ua), combine(back, ub)
            wa, wb = [down(wa, k) for k in range(8)], [down(wb, k) for k in range(8)]
            for g in range(p + 1, groups):
                factors = [across(left[g], 8 * p + k) for k in range(8)]
                left[g] = left[g] - sum(f * w for f, w in zip(factors, wa))
                right[g] = right[g] - sum(f * w for f, w in zip(factors, wb))
    return jnp.concatenate(done, 0)


def final_kernel(row_total, gram_in, *refs):
    parts = refs[:STEPS + 1]
    basis_ref, gram_ref, mix_ref, stage_ref, sems = refs[STEPS + 1:]
    width = gram_ref.shape[0]

    if True:
        groups = [gram_in[:, gram_place(k)] * (1.0 / row_total) for k in range(STEPS + 1)]
        lower = jnp.concatenate(
            [jnp.concatenate([g, jnp.zeros((16, 128 - g.shape[1]), F32)], 1) for g in groups], 0)
        row = lax.broadcasted_iota(jnp.int32, lower.shape, 0)
        lane = lax.broadcasted_iota(jnp.int32, lower.shape, 1)
        lower = jnp.where(row >= lane, lower, 0.0)
        strict = jnp.where(row > lane, lower, 0.0)
        square = jnp.concatenate([strict, jnp.zeros((128 - width, 128), F32)], 0)
        full = lower + square.T[:width]
        gram_ref[...] = full[:, :width]
        inverse = inverse_factor(full)
        high, low = split(inverse[:, :width])
        mix_ref[...] = jnp.concatenate([high, low, high], 1)

    pieces = stage_ref.shape[0]
    chunk = stage_ref.shape[2]

    def out(k):
        return pltpu.make_async_copy(stage_ref.at[k], basis_ref.at[:, pl.ds(k * chunk, chunk)], sems.at[k])

    mix = mix_ref[...]
    for k in range(pieces):
        at = slice(k * chunk, (k + 1) * chunk)
        tops = [p[:16, at] for p in parts]
        lows = [p[16:, at] for p in parts]
        stack = jnp.concatenate(tops + tops + lows, 0)
        stage_ref[k] = jnp.dot(mix, stack, preferred_element_type=F32)
        out(k).start()
    for k in range(pieces):
        out(k).wait()


def params(mib, **kw):
    return pltpu.CompilerParams(vmem_limit_bytes=mib * 2**20, **kw)


def body(start_vectors, tile_index, tile_values, tile_count, ghost_send):
    rows, width = start_vectors.shape
    total, side, _ = tile_values.shape
    blocks = rows // side
    half = ghost_send.shape[2]
    n = lax.axis_size(AXIS)
    basis = width * (STEPS + 1)
    shape = jax.ShapeDtypeStruct

    scaled_t = shape((blocks, width, side), BF16)
    send_t = shape((half, width, side), BF16)
    vec_t = shape((width, rows), F32)
    part_t = shape((2 * width, rows), BF16)
    acc_t = shape((blocks + 1, width, side), F32)
    gram_t = shape((16, 256), F32)

    near = [(i, i ^ 1) for i in range(n)]
    far = [(i, (i + 1) % n if i % 2 else (i - 1) % n) for i in range(n)]

    start = start_vectors.T
    tiles, plan, scale, scaled, send_a, send_b = pl.pallas_call(
        setup_kernel,
        out_shape=(shape((total, side, side), BF16), SMEM((5 * LIST,), jnp.int32),
                   shape((blocks, 8, side), F32), scaled_t, send_t, send_t),
        in_specs=[spec(pltpu.HBM)] * 4 + [spec(SMEM)],
        out_specs=(spec(VMEM), spec(SMEM), spec(VMEM), spec(VMEM), spec(VMEM), spec(VMEM)),
        scratch_shapes=[VMEM((blocks + 1, 8, side), F32), SMEM((2, total), jnp.int32),
                        SMEM((2, half), jnp.int32), VMEM((width, rows), F32), pltpu.SemaphoreType.DMA((len(CHUNKS) + 2,))],
        compiler_params=params(41),
        name="setup",
    )(*[pltpu.with_memory_space_constraint(v, pltpu.HBM)
        for v in (tile_index.T, ghost_send[0], tile_values, start)], tile_count)

    vectors = [start]
    parts = []
    gram = None
    for level in range(1, STEPS + 1):
        last = level == STEPS
        got_a = lax.ppermute(send_a, AXIS, near)
        got_b = lax.ppermute(send_b, AXIS, far)
        args = [plan, tiles, scaled, got_a, vectors[-1]] + parts + ([gram] if gram is not None else [])
        acc, part, gram = pl.pallas_call(
            functools.partial(own_kernel, level - 1),
            out_shape=(acc_t, part_t, gram_t),
            in_specs=[spec(SMEM)] + [spec(VMEM)] * (len(args) - 1),
            out_specs=(spec(VMEM),) * 3,
            compiler_params=params(20),
            cost_estimate=pl.CostEstimate(flops=10**9, bytes_accessed=10**7, transcendentals=0),
            name="own",
        )(*args)
        parts.append(part)
        args = [plan, tiles, got_b, acc, scale]
        if level > 1:
            args.append(vectors[-2])
        if last:
            args += parts + [gram]
            outs = (part_t, gram_t, acc_t)
        else:
            outs = (vec_t, scaled_t, send_t, send_t, acc_t)
        got = pl.pallas_call(
            functools.partial(far_kernel, level, last),
            out_shape=outs,
            in_specs=[spec(SMEM)] + [spec(VMEM)] * (len(args) - 1),
            out_specs=(spec(VMEM),) * len(outs),
            input_output_aliases={3: len(outs) - 1},
            compiler_params=params(20),
            name="far",
        )(*args)
        if last:
            part, gram, _ = got
            parts.append(part)
        else:
            vec, scaled, send_a, send_b, _ = got
            vectors.append(vec)

    def phase(value, shift, count, upward):
        mask = (count - 1) << shift
        moved = value
        for d in range(count - 1, 0, -1):
            perm = []
            for i in range(n):
                step = d if upward(i) else count - d
                perm.append((i, (i & ~mask) | ((((i >> shift) + step) & (count - 1)) << shift)))
            moved = moved + lax.ppermute(value, AXIS, perm)
        return moved

    def high_z(i):
        return i >= n // 2

    def high_y(i):
        return (i >> 4) & 1 == 1

    for shift, count, upward in ((0, 2, high_z), (1, 4, high_z), (3, 4, high_z), (5, 4, high_y)):
        gram = phase(gram, shift, count, upward)

    chunk = 1024
    basis_out, gram_matrix = pl.pallas_call(
        functools.partial(final_kernel, rows * n),
        out_shape=(shape((basis, rows), F32), shape((basis, basis), F32)),
        in_specs=[spec(VMEM)] * (STEPS + 2),
        out_specs=(spec(pltpu.HBM), spec(VMEM)),
        scratch_shapes=[VMEM((basis, 3 * basis), BF16), VMEM((rows // chunk, basis, chunk), F32),
                        pltpu.SemaphoreType.DMA((rows // chunk,))],
        compiler_params=params(20),
        name="final",
    )(gram, *parts)
    return basis_out.T, gram_matrix


def solution(mesh):
    placed = (
        P("parts", None),
        P("parts", None),
        P("parts", None, None),
        P("parts"),
        P("parts", None, None),
    )
    return jax.shard_map(
        body, mesh=mesh, in_specs=placed, out_specs=(P("parts", None), P()), check_vma=False
    )
```
